32 devices in a mesh: groups: 2 (over y), dp: 4 (over x, core), tensor: 4 (over z).
Axes of the slice: x: 2, y: 2, z: 4, core: 2. Of those that a mesh axis runs over, the one named last changes fastest.
Arguments:
- activations: bfloat16 [8192, 8192], P(('groups', 'dp'), 'tensor'), parts along dimension 0, may hold values from -6 to 6
- output_gradient: bfloat16 [8192, 1024], P(('groups', 'dp'), 'tensor'), parts along dimension 0, may hold values from -6 to 6
- value_weight: bfloat16 [8192, 1024], P('tensor'), may hold values from -0.0625 to 0.0625
- adapter_down_factors: float32 [8, 8192, 128], P(('groups', 'dp'), 'tensor'), parts along dimension 0, may hold values from -0.0625 to 0.0625
- adapter_up_factors: float32 [8, 128, 1024], P(('groups', 'dp'), 'tensor'), parts along dimension 0, may hold values from -0.5 to 0.5
- down_first_moment: float32 [8, 8192, 128], P(('groups', 'dp'), 'tensor'), parts along dimension 0, may hold values from -0.12 to 0.12
- down_second_moment: float32 [8, 8192, 128], P(('groups', 'dp'), 'tensor'), parts along dimension 0, may hold values from 1e-05 to 0.001
- up_first_moment: float32 [8, 128, 1024], P(('groups', 'dp'), 'tensor'), parts along dimension 0, may hold values from -0.12 to 0.12
- up_second_moment: float32 [8, 128, 1024], P(('groups', 'dp'), 'tensor'), parts along dimension 0, may hold values from 1e-05 to 0.001
- block_tenant: int32 [128], P(('groups', 'dp')), parts along dimension 0, may hold values from 0 to 3
- block_live_tokens: int32 [128], P(('groups', 'dp')), parts along dimension 0, may hold values from 1 to 64, as said below
- tenant_storage_slot: int32 [8], P('groups'), parts along dimension 0, may hold values from 0 to 3, each once
- tenant_adapter_rank: int32 [8], P('groups'), parts along dimension 0, may hold values from 8 to 128
Outputs:
- grad_acts: bfloat16 [8192, 8192], P(('groups', 'dp'), 'tensor'), parts along dimension 0
- updated_down_factors: float32 [8, 8192, 128], P(('groups', 'dp'), 'tensor'), parts along dimension 0
- updated_down_first: float32 [8, 8192, 128], P(('groups', 'dp'), 'tensor'), parts along dimension 0
- updated_down_second: float32 [8, 8192, 128], P(('groups', 'dp'), 'tensor'), parts along dimension 0
- updated_up_factors: float32 [8, 128, 1024], P(('groups', 'dp'), 'tensor'), parts along dimension 0
- updated_up_first: float32 [8, 128, 1024], P(('groups', 'dp'), 'tensor'), parts along dimension 0
- updated_up_second: float32 [8, 128, 1024], P(('groups', 'dp'), 'tensor'), parts along dimension 0
The draws below stay inside these ranges and needn't reach their ends.
There are 2 independent parts, one for each index of `groups`. The reference program is written for one: setup_inputs(seed, part) draws one part's arguments, and reference() takes and returns one part's arrays. A program takes and returns all parts, laid end to end along the dimension named above; an argument that names none is the same for every part. Nothing has to cross between parts.
Inputs may be any that keep to these rules, and one draw needn't show every extreme that they name: `block_live_tokens`: among the 16 blocks of each index of dp at least one is live in all 64 slots.
All inputs are finite; a program needn't handle non-finite values.
Results may differ from the reference program's by a relative error of at most 0.012.
Values may be sent and summed in bfloat16 or wider, within the bound.
No kernel may reach another device: no remote copies, remote signals or barrier semaphores. Data moves between devices by JAX's collectives and lax.ppermute only.
A program may use at most 128 MiB of HBM per device.

```python
import math
import jax
import jax.numpy as jnp
import numpy as np
from jax import lax

MODEL_WIDTH = 8192
VALUE_WIDTH = 1024
LARGEST_RANK = 128
BLK_LEN = 64
BLK_DEV = 16
TENANT_TOTAL = 4
BLOCKS = 64
TOKENS = 4096
N_DP = 4


def draw_block_live_tokens(key, part):
    key = jax.random.fold_in(key, 11)
    first_key, second_key = jax.random.split(key)
    lengths = jax.random.randint(first_key, (BLOCKS,), 1, BLK_LEN + 1)
    replicas = BLOCKS // BLK_DEV
    chosen = jax.random.randint(second_key, (replicas,), 0, BLK_DEV)
    filled = jnp.arange(BLOCKS) % BLK_DEV == jnp.repeat(chosen, BLK_DEV, total_repeat_length=BLOCKS)
    return jnp.where(filled, BLK_LEN, lengths).astype(jnp.int32)


def touch_ends(entries, stream_key, least, top_value):
    spot = [jax.random.randint(jax.random.fold_in(stream_key, axis), (), 0, length) for axis, length in enumerate(entries.shape)]
    main_axis = entries.shape.index(max(entries.shape))
    neighbour = spot[:main_axis] + [(spot[main_axis] + 1) % entries.shape[main_axis]] + spot[main_axis + 1:]
    return entries.at[tuple(spot)].set(least).at[tuple(neighbour)].set(top_value)


def block_scale(rng, dims, pieces, smallest, top_value):
    gain = 1.0
    for axis_at, blocks in pieces:
        heights = jax.random.uniform(jax.random.fold_in(jax.random.fold_in(rng, 6), axis_at), (blocks,), jnp.float32, smallest / len(pieces), top_value / len(pieces))
        gain = gain * jnp.repeat(jnp.exp(heights), dims[axis_at] // blocks).reshape((-1,) + (1,) * (len(dims) - 1 - axis_at))
    return gain


def rank_table(amount, slope):
    weights = [(1 << 20) // math.isqrt(standing ** slope) + 1 for standing in range(1, amount + 1)]
    scale = 1 + sum(weights) // (1 << 30)
    return np.cumsum(np.array([max(1, weight // scale) for weight in weights]))


def ranked_ids(stream_key, dims, count, skew):
    listing = rank_table(count, skew)
    lot = jax.random.randint(jax.random.fold_in(stream_key, 1), dims, 0, int(listing[count - 1]))
    rank = jnp.searchsorted(jnp.asarray(listing, jnp.int32), lot, side="right")
    return jax.random.permutation(jax.random.fold_in(stream_key, 2), count)[rank].astype(jnp.int32)


def gaussian(rng, shape, scale, most, pieces=(), kind=jnp.bfloat16):
    values = scale * jax.random.normal(rng, shape, jnp.float32)
    if pieces:
        values = values * block_scale(rng, shape, pieces, -0.22, 0.18)
    return jnp.clip(values, -most, most).astype(kind)


def setup_inputs(seed: int = 0, part: int = 0) -> dict:
    keys = jax.random.split(jax.random.key(seed), 14)
    own_keys = jax.random.split(jax.random.fold_in(keys[13], part), 14)
    return {
        "activations": gaussian(own_keys[0], (TOKENS, MODEL_WIDTH), 1.0, 6.0, ((0, 4), (1, 4))),
        "output_gradient": gaussian(own_keys[1], (TOKENS, VALUE_WIDTH), 1.0, 6.0, ((0, 4), (1, 4))),
        "value_weight": gaussian(keys[2], (MODEL_WIDTH, VALUE_WIDTH), MODEL_WIDTH ** -0.5, 0.0625, ((0, 4),)),
        "adapter_down_factors": gaussian(own_keys[3], (TENANT_TOTAL, MODEL_WIDTH, LARGEST_RANK), MODEL_WIDTH ** -0.5, 0.0625, ((0, 4), (1, 4)), jnp.float32),
        "adapter_up_factors": gaussian(own_keys[4], (TENANT_TOTAL, LARGEST_RANK, VALUE_WIDTH), LARGEST_RANK ** -0.5, 0.5, ((0, 4), (1, 4)), jnp.float32),
        "down_first_moment": gaussian(own_keys[5], (TENANT_TOTAL, MODEL_WIDTH, LARGEST_RANK), 0.02, 0.12, ((0, 4), (1, 4)), jnp.float32),
        "down_second_moment": jnp.clip(jnp.exp(math.log(0.001) - 4.6051703 * jax.random.uniform(own_keys[6], (TENANT_TOTAL, MODEL_WIDTH, LARGEST_RANK), jnp.float32) ** block_scale(own_keys[6], (TENANT_TOTAL, MODEL_WIDTH, LARGEST_RANK), ((0, 4), (1, 4)), -0.2, 0.2)), 9.999999747378752e-06, 0.001),
        "up_first_moment": gaussian(own_keys[7], (TENANT_TOTAL, LARGEST_RANK, VALUE_WIDTH), 0.02, 0.12, ((0, 4), (1, 4)), jnp.float32),
        "up_second_moment": jnp.clip(jnp.exp(math.log(0.001) - 4.6051703 * jax.random.uniform(own_keys[8], (TENANT_TOTAL, LARGEST_RANK, VALUE_WIDTH), jnp.float32) ** block_scale(own_keys[8], (TENANT_TOTAL, LARGEST_RANK, VALUE_WIDTH), ((0, 4), (1, 4)), -0.2, 0.2)), 9.999999747378752e-06, 0.001),
        "block_tenant": touch_ends(ranked_ids(own_keys[9], (BLOCKS,), TENANT_TOTAL, 3), jax.random.fold_in(own_keys[9], 3), 0, TENANT_TOTAL - 1).astype(jnp.int32),
        "block_live_tokens": draw_block_live_tokens(jax.random.fold_in(jax.random.fold_in(keys[13], part), 71), part),
        "tenant_storage_slot": jax.random.permutation(own_keys[11], TENANT_TOTAL).astype(jnp.int32),
        "tenant_adapter_rank": touch_ends(jax.random.randint(own_keys[12], (TENANT_TOTAL,), LARGEST_RANK // 16, LARGEST_RANK + 1), jax.random.fold_in(own_keys[12], 1), LARGEST_RANK // 16, LARGEST_RANK).astype(jnp.int32),
    }


highest = lax.Precision.HIGHEST
adapter_alpha_scale = 16.0
beta_one = 0.9
beta_two = 0.999
adam_eps = 1e-08
learn_rate = 0.001
adam_step = 10

def moment_update_rule(param, first, second, grad):
    new_first = beta_one * first + (1.0 - beta_one) * grad
    new_second = beta_two * second + (1.0 - beta_two) * grad * grad
    fixed_first = new_first / (1.0 - beta_one ** adam_step)
    fixed_second = new_second / (1.0 - beta_two ** adam_step)
    return (param - learn_rate * fixed_first / (jnp.sqrt(fixed_second) + adam_eps), new_first, new_second)

def reference(activations, output_gradient, value_weight, adapter_down_factors, adapter_up_factors, down_first_moment, down_second_moment, up_first_moment, up_second_moment, block_tenant, block_live_tokens, tenant_storage_slot, tenant_adapter_rank):
    tenants = tenant_storage_slot.shape[0]
    blocks = block_tenant.shape[0]
    blk_dev = blocks // N_DP
    blk_len = activations.shape[0] // blocks
    largest_adapter_rank = adapter_down_factors.shape[2]
    width = activations.shape[1]
    value_output_width = output_gradient.shape[1]
    tenant_ids = jnp.arange(tenants, dtype=jnp.int32)
    matches = block_tenant[:, None] == tenant_ids[None, :]
    slot_of = lax.optimization_barrier(jnp.sum(jnp.where(matches, tenant_storage_slot[None, :], 0), axis=1)).astype(jnp.int32)
    block_rank_lookup = lax.optimization_barrier(jnp.sum(jnp.where(matches, tenant_adapter_rank[None, :], 0), axis=1)).astype(jnp.int32)
    tenant_scales = adapter_alpha_scale / block_rank_lookup.astype(jnp.float32)
    col_live = jnp.arange(largest_adapter_rank, dtype=jnp.int32)[None, :] < block_rank_lookup[:, None]
    row_live = jnp.arange(blk_len, dtype=jnp.int32)[None, :] < block_live_tokens[:, None]
    down_factor_half = adapter_down_factors.astype(jnp.bfloat16)
    up_factor_half = adapter_up_factors.astype(jnp.bfloat16)
    zero_half = jnp.zeros((), jnp.bfloat16)
    rows = blk_dev * blk_len

    def replica(carry, replica_at):
        sum_a, sum_b = carry
        first_block = (replica_at * blk_dev).astype(jnp.int32)
        x_blocks = lax.dynamic_slice_in_dim(activations, first_block * blk_len, rows, 0)
        g_blocks = lax.dynamic_slice_in_dim(output_gradient, first_block * blk_len, rows, 0).reshape(blk_dev, blk_len, value_output_width)
        slots_here = lax.dynamic_slice_in_dim(slot_of, first_block, blk_dev, 0)
        cols_here = lax.dynamic_slice_in_dim(col_live, first_block, blk_dev, 0)
        rows_here = lax.dynamic_slice_in_dim(row_live, first_block, blk_dev, 0)
        scale_here = lax.dynamic_slice_in_dim(tenant_scales, first_block, blk_dev, 0)
        cotangent = jnp.where(rows_here[:, :, None], g_blocks, zero_half)
        used_a = jnp.where(cols_here[:, None, :], down_factor_half[slots_here], zero_half)
        used_b = jnp.where(cols_here[:, :, None], up_factor_half[slots_here], zero_half)
        x_wide = x_blocks.astype(jnp.float32).reshape(blk_dev, blk_len, width)
        cot_wide = cotangent.astype(jnp.float32)
        a_wide = used_a.astype(jnp.float32)
        hidden = jnp.einsum('bpd,bdr->bpr', x_wide, a_wide, precision=highest)
        upward = jnp.einsum('bpk,brk->bpr', cot_wide, used_b.astype(jnp.float32), precision=highest)
        scaled_u = (upward * scale_here[:, None, None]).astype(jnp.bfloat16).astype(jnp.float32)
        scaled_h = (hidden * scale_here[:, None, None]).astype(jnp.bfloat16).astype(jnp.float32)
        base = jnp.dot(cotangent.reshape(rows, value_output_width), value_weight.T, preferred_element_type=jnp.float32)
        adapter = jnp.einsum('bpr,bdr->bpd', scaled_u, a_wide, precision=highest).reshape(rows, width)
        grad_rows = (base + adapter).astype(jnp.bfloat16)
        slot_match = (slots_here[:, None] == tenant_ids[None, :]).astype(jnp.float32)
        block_a = jnp.einsum('bpd,bpr->bdr', x_wide, scaled_u, precision=highest)
        block_b = jnp.einsum('bpr,bpk->brk', scaled_h, cot_wide, precision=highest)
        part_a = jnp.einsum('bt,bdr->tdr', slot_match, block_a, precision=highest).astype(jnp.bfloat16)
        part_b = jnp.einsum('bt,brk->trk', slot_match, block_b, precision=highest).astype(jnp.bfloat16)
        part_a = lax.optimization_barrier(part_a).astype(jnp.float32)
        part_b = lax.optimization_barrier(part_b).astype(jnp.float32)
        return ((sum_a + part_a, sum_b + part_b), grad_rows)
    start_offset = (jnp.zeros(adapter_down_factors.shape, jnp.float32), jnp.zeros(adapter_up_factors.shape, jnp.float32))
    sums, grad_stack = lax.scan(replica, start_offset, jnp.arange(N_DP, dtype=jnp.int32))
    grad_acts = grad_stack.reshape(-1, width)
    live_count = lax.optimization_barrier(jnp.sum(jnp.where(matches, block_live_tokens[:, None], 0), axis=0)).astype(jnp.float32)
    count_slot = lax.optimization_barrier(jnp.sum(jnp.where(tenant_storage_slot[:, None] == tenant_ids[None, :], live_count[:, None], jnp.float32(0.0)), axis=0))
    denom = jnp.maximum(count_slot, 1.0)
    down_factor_gradient = sums[0] / denom[:, None, None]
    up_factor_gradient = sums[1] / denom[:, None, None]
    updated_down_factors, updated_down_first, updated_down_second = moment_update_rule(adapter_down_factors, down_first_moment, down_second_moment, down_factor_gradient)
    updated_up_factors, updated_up_first, updated_up_second = moment_update_rule(adapter_up_factors, up_first_moment, up_second_moment, up_factor_gradient)
    return (grad_acts, updated_down_factors, updated_down_first, updated_down_second, updated_up_factors, updated_up_first, updated_up_second)
```

```python
import functools

import jax
import jax.numpy as jnp
from jax import lax
from jax.experimental import pallas as pl
from jax.experimental.pallas import tpu as pltpu
from jax.sharding import PartitionSpec as P

adapter_alpha_scale = 16.0
beta_one = 0.9
beta_two = 0.999
adam_eps = 1e-08
learn_rate = 0.001
adam_step = 10
half = jnp.bfloat16
wide = jnp.float32
MIB = 1 << 20
NT = (((1,), (1,)), ((), ()))
TN = (((0,), (0,)), ((), ()))
NN = (((1,), (0,)), ((), ()))


def mm(a, b, dims):
    return lax.dot_general(a, b, dims, preferred_element_type=wide)


def moment_update_rule(param, first, second, grad):
    new_first = beta_one * first + (1.0 - beta_one) * grad
    new_second = beta_two * second + (1.0 - beta_two) * grad * grad
    fixed_first = new_first / (1.0 - beta_one**adam_step)
    fixed_second = new_second / (1.0 - beta_two**adam_step)
    return (
        param - learn_rate * fixed_first / (jnp.sqrt(fixed_second) + adam_eps),
        new_first,
        new_second,
    )


def bit_order(n):
    if n == 1:
        return [0]
    inner = [2 * i for i in bit_order(n // 2)]
    return inner + [i + 1 for i in inner]


def line_ring(n):
    return [0] + list(range(1, n, 2)) + list(range(n - 2 + n % 2, 0, -2))


def swap(v, axis, n, bits):
    return lax.ppermute(v, axis, [(i, i ^ bits) for i in range(n)])


def kernel_params(mib):
    return pltpu.CompilerParams(vmem_limit_bytes=mib * MIB)


def cost(flops, nbytes):
    return pl.CostEstimate(flops=int(flops), bytes_accessed=int(nbytes), transcendentals=0)


def hidden_kernel(order, ranks, x_ref, even_ref, odd_ref, info_ref, out_ref):
    slot = info_ref[0:1, :]
    x = x_ref[...]
    total = None
    per = len(order) // 2
    for side, ref in enumerate((even_ref, odd_ref)):
        prod = mm(ref[...], x, NT)
        for i in range(per):
            piece = prod[i * ranks : (i + 1) * ranks]
            piece = jnp.where(slot == float(order[side * per + i]), piece, 0.0)
            total = piece if total is None else total + piece
    out_ref[...] = total.astype(half)


def hidden_call(x, even, odd, info, order, ranks):
    tok, width = x.shape
    blk = min(256, tok)
    return pl.pallas_call(
        functools.partial(hidden_kernel, order, ranks),
        grid=(tok // blk,),
        in_specs=[
            pl.BlockSpec((blk, width), lambda i: (i, 0)),
            pl.BlockSpec(even.shape, lambda i: (0, 0)),
            pl.BlockSpec(odd.shape, lambda i: (0, 0)),
            pl.BlockSpec((info.shape[0], blk), lambda i: (0, i)),
        ],
        out_specs=pl.BlockSpec((ranks, blk), lambda i: (0, i)),
        out_shape=jax.ShapeDtypeStruct((ranks, tok), half),
        compiler_params=kernel_params(32),
        cost_estimate=cost(2 * tok * width * ranks * len(order), 2 * (x.size + 2 * even.size)),
        name="hidden",
    )(x, even, odd, info)


def upward_kernel(parts, src_ref, *refs):
    cots, (even_ref, odd_ref, coef_ref, out_ref) = refs[:parts], refs[parts:]
    kw = cots[0].shape[1]
    rows = cots[0].shape[0]
    per = even_ref.shape[0]
    blocks = coef_ref.shape[0]
    for side, ref in enumerate((even_ref, odd_ref)):
        acc = None
        for i in range(parts):
            cols = pl.ds(pl.multiple_of(src_ref[i] * kw, kw), kw)
            prod = mm(cots[i][...], ref[:, cols], NT)
            acc = prod if acc is None else acc + prod
        coef = coef_ref[:, :, side * per : (side + 1) * per]
        acc = acc.reshape(blocks, rows // blocks, per) * coef
        out_ref[:, side * per : (side + 1) * per] = acc.reshape(rows, per).astype(half)


def upward_call(cots, even, odd, coef, src):
    rows, kw = cots[0].shape
    per = even.shape[0]
    blocks = coef.shape[0]
    return pl.pallas_call(
        functools.partial(upward_kernel, len(cots)),
        grid_spec=pltpu.PrefetchScalarGridSpec(
            num_scalar_prefetch=1,
            grid=(1,),
            in_specs=[pl.BlockSpec((rows, kw), lambda i, s: (0, 0))] * len(cots)
            + [
                pl.BlockSpec(even.shape, lambda i, s: (0, 0)),
                pl.BlockSpec(odd.shape, lambda i, s: (0, 0)),
                pl.BlockSpec(coef.shape, lambda i, s: (0, 0, 0)),
            ],
            out_specs=pl.BlockSpec((rows, 2 * per), lambda i, s: (0, 0)),
        ),
        out_shape=jax.ShapeDtypeStruct((rows, 2 * per), half),
        compiler_params=kernel_params(32),
        cost_estimate=cost(4 * rows * kw * len(cots) * per, 2 * (rows * kw * len(cots) + 2 * even.size)),
        name="upward",
    )(src, *cots, even, odd, coef)


def down_kernel(chunks, ranks, *refs):
    x_ref, us, (keep_ref, send_ref) = refs[0], refs[1 : 1 + chunks], refs[1 + chunks :]
    acc = None
    at = 0
    for u in us:
        rows = u.shape[0]
        prod = mm(x_ref[at : at + rows, :], u[...], TN)
        acc = prod if acc is None else acc + prod
        at += rows
    per = keep_ref.shape[0]
    for i in range(per):
        keep_ref[i] = acc[:, i * ranks : (i + 1) * ranks].astype(half)
        send_ref[i] = acc[:, (per + i) * ranks : (per + i + 1) * ranks].astype(half)


def down_call(x, us, ranks, start, count):
    tok = x.shape[0]
    slots = us[0].shape[1] // ranks
    blk = min(512, count)
    shape = jax.ShapeDtypeStruct((slots // 2, count, ranks), half)
    first = start // blk
    return pl.pallas_call(
        functools.partial(down_kernel, len(us), ranks),
        grid=(count // blk,),
        in_specs=[pl.BlockSpec((tok, blk), lambda i: (0, first + i))]
        + [pl.BlockSpec(u.shape, lambda i: (0, 0)) for u in us],
        out_specs=[pl.BlockSpec((slots // 2, blk, ranks), lambda i: (0, i, 0))] * 2,
        out_shape=[shape, shape],
        compiler_params=kernel_params(32),
        cost_estimate=cost(2 * tok * count * slots * ranks, 2 * (tok * count + slots * ranks * (tok + count))),
        name="down_grad",
    )(x, *us)


def up_kernel(order, chunks, parts, n_hs, extra, src_ref, *refs):
    hs = refs[:n_hs]
    info_ref, counts_ref = refs[n_hs : n_hs + 2]
    cots = refs[n_hs + 2 : n_hs + 2 + chunks * parts]
    keep_ref, send_ref = refs[n_hs + 2 + chunks * parts :]
    own = hs[0].shape[0]
    per = len(order) // 2
    total = hs[0][...].astype(wide)
    for h in hs[1:]:
        total = total + h[...].astype(wide)
    rank_at = src_ref[parts] * own + lax.broadcasted_iota(jnp.int32, total.shape, 0)
    slot, rank, scale = info_ref[0:1, :], info_ref[1:2, :], info_ref[2:3, :]
    total = jnp.where(rank_at.astype(wide) < rank, total * scale, 0.0).astype(half)
    lhs = jnp.concatenate(
        [jnp.where(slot == float(j), total, jnp.zeros_like(total)) for j in order], axis=0
    )
    for i in range(parts):
        acc = None
        at = 0
        for c in range(chunks):
            cot = cots[c * parts + i]
            prod = mm(lhs[:, at : at + cot.shape[0]], cot[...], NN)
            acc = prod if acc is None else acc + prod
            at += cot.shape[0]
        kw = acc.shape[1]
        cols = pl.ds(pl.multiple_of(src_ref[i] * kw, kw), kw)
        acc = acc.astype(half)
        for k in range(per):
            keep_ref[k, :own, cols] = acc[k * own : (k + 1) * own]
            send_ref[k, :own, cols] = acc[(per + k) * own : (per + k + 1) * own]
    row = lax.broadcasted_iota(jnp.int32, (extra, keep_ref.shape[2]), 0)
    for k in range(per):
        for ref, at in ((keep_ref, k), (send_ref, per + k)):
            tail = jnp.where(row == 0, counts_ref[0, at], jnp.where(row == 1, counts_ref[1, at], 0.0))
            ref[k, own:, :] = tail.astype(half)


def up_call(hs, info, counts, chunk_cots, src, order, extra=16):
    parts = len(chunk_cots[0])
    own, tok = hs[0].shape
    cots = [c for chunk in chunk_cots for c in chunk]
    kw = cots[0].shape[1]
    shape = jax.ShapeDtypeStruct((len(order) // 2, own + extra, kw * parts), half)
    whole = lambda a: pl.BlockSpec(a.shape, lambda i, s, n=len(a.shape): (0,) * n)
    return pl.pallas_call(
        functools.partial(up_kernel, order, len(chunk_cots), parts, len(hs), extra),
        grid_spec=pltpu.PrefetchScalarGridSpec(
            num_scalar_prefetch=1,
            grid=(1,),
            in_specs=[whole(h) for h in hs]
            + [whole(info), pl.BlockSpec(memory_space=pltpu.SMEM)]
            + [whole(c) for c in cots],
            out_specs=[whole(shape)] * 2,
        ),
        out_shape=[shape, shape],
        compiler_params=kernel_params(32),
        cost_estimate=cost(2 * len(order) * own * tok * kw * parts, 4 * tok * kw * parts),
        name="up_grad",
    )(src, *hs, info, counts, *cots)


def up_plain(hs, info, counts, chunk_cots, z, order, extra=16):
    own = hs[0].shape[0]
    total = sum(h.astype(wide) for h in hs)
    rank_at = (z * own + jnp.arange(own, dtype=jnp.int32)).astype(wide)
    total = jnp.where(rank_at[:, None] < info[1:2], total * info[2:3], 0.0).astype(half)
    lhs = jnp.concatenate([jnp.where(info[0:1] == float(j), total, 0) for j in order], axis=0)
    cot = jnp.concatenate([chunk[0] for chunk in chunk_cots], axis=0)
    grads = mm(lhs, cot, NN).astype(half).reshape(len(order), own, cot.shape[1])
    tail = jnp.pad(counts.T, ((0, 0), (0, extra - 2))).astype(half)[:, :, None]
    tail = jnp.broadcast_to(tail, (len(order), extra, cot.shape[1]))
    both = jnp.concatenate([grads, tail], axis=1)
    return both[: len(order) // 2], both[len(order) // 2 :]


def acts_kernel(chunks, parts, src_ref, *refs):
    w_ref, even_ref, odd_ref = refs[:3]
    cots = refs[3 : 3 + chunks * parts]
    us = refs[3 + chunks * parts : 3 + chunks * parts + chunks]
    out_ref = refs[-1]
    per = even_ref.shape[0]
    at = 0
    for c in range(chunks):
        rows = us[c].shape[0]
        acc = mm(us[c][:, :per], even_ref[...], NN) + mm(us[c][:, per:], odd_ref[...], NN)
        for i in range(parts):
            cot = cots[c * parts + i]
            kw = cot.shape[1]
            cols = pl.ds(pl.multiple_of(src_ref[i] * kw, kw), kw)
            acc = acc + mm(cot[...], w_ref[:, cols], NT)
        out_ref[at : at + rows, :] = acc.astype(half)
        at += rows


def acts_call(w, even, odd, chunk_cots, us, src):
    width, kfull = w.shape
    per = even.shape[0]
    parts = len(chunk_cots[0])
    tok = sum(u.shape[0] for u in us)
    blk = min(512, width)
    cots = [c for chunk in chunk_cots for c in chunk]
    whole = lambda a: pl.BlockSpec(a.shape, lambda i, s: (0, 0))
    return pl.pallas_call(
        functools.partial(acts_kernel, len(us), parts),
        grid_spec=pltpu.PrefetchScalarGridSpec(
            num_scalar_prefetch=1,
            grid=(width // blk,),
            in_specs=[
                pl.BlockSpec((blk, kfull), lambda i, s: (i, 0)),
                pl.BlockSpec((per, blk), lambda i, s: (0, i)),
                pl.BlockSpec((per, blk), lambda i, s: (0, i)),
            ]
            + [whole(c) for c in cots]
            + [whole(u) for u in us],
            out_specs=pl.BlockSpec((tok, blk), lambda i, s: (0, i)),
        ),
        out_shape=jax.ShapeDtypeStruct((tok, width), half),
        compiler_params=kernel_params(40),
        cost_estimate=cost(2 * tok * width * (kfull + 2 * per), 2 * (w.size + 2 * even.size + tok * (width + kfull))),
        name="grad_acts",
    )(src, w, even, odd, *cots, *us)


def shards(
    n_dp,
    n_tensor,
    activations,
    output_gradient,
    value_weight,
    adapter_down_factors,
    adapter_up_factors,
    down_first_moment,
    down_second_moment,
    up_first_moment,
    up_second_moment,
    block_tenant,
    block_live_tokens,
    tenant_storage_slot,
    tenant_adapter_rank,
):
    tok, width = activations.shape
    blocks = block_tenant.shape[0]
    blk_len = tok // blocks
    slots = tenant_storage_slot.shape[0]
    assert adapter_down_factors.shape[0] == 1 and slots == n_dp
    ranks = adapter_down_factors.shape[2]
    own_ranks = adapter_up_factors.shape[1]
    value_width = adapter_up_factors.shape[2]
    z = lax.axis_index("tensor")
    d = lax.axis_index("dp")
    order = bit_order(slots)
    levels = [1 << b for b in range(slots.bit_length() - 1)]

    tenant_ids = jnp.arange(slots, dtype=jnp.int32)
    matches = block_tenant[:, None] == tenant_ids[None, :]
    slot_of = jnp.sum(jnp.where(matches, tenant_storage_slot[None, :], 0), axis=1)
    rank_of = jnp.sum(jnp.where(matches, tenant_adapter_rank[None, :], 0), axis=1)
    scale_of = adapter_alpha_scale / rank_of.astype(wide)
    near_of = jnp.bitwise_xor(slot_of, d)
    order_row = jnp.array(order, jnp.int32)
    hit = near_of[:, None] == order_row[None, :]
    rank_live = jnp.arange(ranks, dtype=jnp.int32)[None, :] < rank_of[:, None]
    coef = jnp.where(hit[:, :, None] & rank_live[:, None, :], scale_of[:, None, None], 0.0)
    coef = coef.reshape(blocks, 1, slots * ranks)
    info = jnp.stack([near_of.astype(wide), rank_of.astype(wide), scale_of], axis=0)
    info = jnp.repeat(jnp.pad(info, ((0, 5), (0, 0))), blk_len, axis=1)
    counts = jnp.sum(jnp.where(hit, block_live_tokens[:, None], 0), axis=0)
    counts = jnp.stack([counts // 32, counts % 32]).astype(wide)
    row_live = jnp.arange(blk_len, dtype=jnp.int32)[None, :] < block_live_tokens[:, None]

    ring = line_ring(n_tensor)
    ring_at = [ring.index(i) for i in range(n_tensor)]
    ring_pairs = [(ring[i], ring[(i + 1) % n_tensor]) for i in range(n_tensor)]
    place = jnp.array(ring_at, jnp.int32)[z]
    src = jnp.array(ring, jnp.int32)[(place - jnp.arange(n_tensor, dtype=jnp.int32)) % n_tensor]
    src = jnp.concatenate([src, z.astype(jnp.int32)[None]])
    masked = jnp.where(row_live.reshape(tok, 1), output_gradient, jnp.zeros((), half))
    chunks = 2
    chunk_rows = tok // chunks
    chunk_cots = []
    for c in range(chunks):
        chunk_cots.append([masked[c * chunk_rows : (c + 1) * chunk_rows]])
    for _ in range(n_tensor - 1):
        for c in range(chunks):
            chunk_cots[c].append(lax.ppermute(chunk_cots[c][-1], "tensor", ring_pairs))

    if output_gradient.shape[1] % 128:
        away = (place - jnp.array(ring_at, jnp.int32)) % n_tensor
        chunk_cots = [
            [jnp.moveaxis(jnp.stack(c)[away], 0, 1).reshape(chunk_rows, value_width)]
            for c in chunk_cots
        ]
        src = jnp.concatenate([jnp.zeros((1,), jnp.int32), src[-1:]])

    even_a = adapter_down_factors[0].astype(half).T
    for bits in reversed(levels[1:]):
        even_a = jnp.concatenate([even_a, swap(even_a, "dp", n_dp, bits)], axis=0)
    odd_a = swap(even_a, "dp", n_dp, 1)

    own_b = adapter_up_factors[0].astype(half)
    pieces = jnp.stack([own_b] + [swap(own_b, "tensor", n_tensor, k) for k in range(1, n_tensor)])
    even_b = pieces[jnp.bitwise_xor(z, jnp.arange(n_tensor))].reshape(ranks, value_width)
    for bits in reversed(levels[1:]):
        even_b = jnp.concatenate([even_b, swap(even_b, "dp", n_dp, bits)], axis=0)
    odd_b = swap(even_b, "dp", n_dp, 1)

    hidden_part = hidden_call(activations, even_a, odd_a, info, order, ranks)
    hs = [lax.dynamic_slice_in_dim(hidden_part, z * own_ranks, own_ranks, 0)]
    for k in range(1, n_tensor):
        theirs = lax.dynamic_slice_in_dim(
            hidden_part, jnp.bitwise_xor(z, k) * own_ranks, own_ranks, 0
        )
        hs.append(swap(theirs, "tensor", n_tensor, k))

    per_chunk = blocks // chunks
    us = [
        upward_call(chunk_cots[c], even_b, odd_b, coef[c * per_chunk : (c + 1) * per_chunk], src)
        for c in range(chunks)
    ]

    def scatter(keep, send):
        total = keep.astype(wide) + swap(send, "dp", n_dp, 1).astype(wide)
        for bits in levels[1:]:
            n = total.shape[0] // 2
            total = total[:n] + swap(total[n:].astype(half), "dp", n_dp, bits).astype(wide)
        return total[0]

    down_sums = []
    pieces_down = 2
    for p in range(pieces_down):
        rows = width // pieces_down
        keep, send = down_call(activations, us, ranks, p * rows, rows)
        down_sums.append(scatter(keep, send))
    if own_ranks % 16:
        keep, send = up_plain(hs, info, counts, chunk_cots, z, order)
    else:
        keep, send = up_call(hs, info, counts, chunk_cots, src, order)
    up_sum = scatter(keep, send)
    denom = jnp.maximum(up_sum[own_ranks, 0] * 32.0 + up_sum[own_ranks + 1, 0], 1.0)
    grad_acts = acts_call(value_weight, even_a, odd_a, chunk_cots, us, src)

    down_grad = jnp.concatenate(down_sums, axis=0)[None] / denom
    up_grad = up_sum[None, :own_ranks] / denom
    return (
        grad_acts,
        *moment_update_rule(adapter_down_factors, down_first_moment, down_second_moment, down_grad),
        *moment_update_rule(adapter_up_factors, up_first_moment, up_second_moment, up_grad),
    )


def solution(mesh):
    tokens = P(("groups", "dp"), "tensor")
    factors = P(("groups", "dp"), "tensor", None)
    placed = (tokens, tokens, P("tensor", None), *([factors] * 6), P(("groups", "dp")), P(("groups", "dp")), P("groups"), P("groups"))
    return jax.shard_map(
        functools.partial(shards, mesh.shape["dp"], mesh.shape["tensor"]),
        mesh=mesh,
        in_specs=placed,
        out_specs=(tokens, *([factors] * 6)),
        check_vma=False,
    )
```

```python
import functools

import jax
import jax.numpy as jnp
from jax import lax
from jax.experimental import pallas as pl
from jax.experimental.pallas import tpu as pltpu
from jax.sharding import PartitionSpec as P

adapter_alpha_scale = 16.0
beta_one = 0.9
beta_two = 0.999
adam_eps = 1e-08
learn_rate = 0.001
adam_step = 10
half = jnp.bfloat16
wide = jnp.float32
MIB = 1 << 20
NT = (((1,), (1,)), ((), ()))
TN = (((0,), (0,)), ((), ()))
NN = (((1,), (0,)), ((), ()))


def mm(a, b, dims):
    return lax.dot_general(a, b, dims, preferred_element_type=wide)


def moment_update_rule(param, first, second, grad):
    new_first = beta_one * first + (1.0 - beta_one) * grad
    new_second = beta_two * second + (1.0 - beta_two) * grad * grad
    fixed_first = new_first / (1.0 - beta_one**adam_step)
    fixed_second = new_second / (1.0 - beta_two**adam_step)
    return (
        param - learn_rate * fixed_first / (jnp.sqrt(fixed_second) + adam_eps),
        new_first,
        new_second,
    )


def bit_order(n):
    if n == 1:
        return [0]
    inner = [2 * i for i in bit_order(n // 2)]
    return inner + [i + 1 for i in inner]


def line_ring(n):
    return [0] + list(range(1, n, 2)) + list(range(n - 2 + n % 2, 0, -2))


def swap(v, axis, n, bits):
    return lax.ppermute(v, axis, [(i, i ^ bits) for i in range(n)])


def kernel_params(mib):
    return pltpu.CompilerParams(vmem_limit_bytes=mib * MIB)


def cost(flops, nbytes):
    return pl.CostEstimate(flops=int(flops), bytes_accessed=int(nbytes), transcendentals=0)


def block_table(refs, b, d):
    tenant_ref, slot_ref, rank_ref = refs
    tenant = tenant_ref[b]
    return jnp.bitwise_xor(slot_ref[tenant], d), rank_ref[tenant]


def inverse_rank(rank, shape):
    return adapter_alpha_scale / jnp.full(shape, rank, jnp.int32).astype(wide)


def sources(z, n):
    ring = line_ring(n)
    out = []
    for i in range(n):
        came = [ring[(ring.index(k) - i) % n] for k in range(n)]
        at = came[0]
        for k in range(1, n):
            at = jnp.where(z == k, came[k], at)
        out.append(at)
    return out


def smem():
    return pl.BlockSpec(memory_space=pltpu.SMEM)


def resident(a):
    return pl.BlockSpec(a.shape, lambda *_, n=len(a.shape): (0,) * n)


def vmem():
    return pl.BlockSpec(memory_space=pltpu.VMEM)


def starts_of(live_ref):
    starts, at = [], 0
    for b in range(live_ref.shape[0]):
        starts.append(at)
        at = at + live_ref[b]
    return starts, at


def stage_kernel(from_ref, to_ref, sem):
    copy = pltpu.make_async_copy(from_ref, to_ref, sem)
    copy.start()
    copy.wait()


def stage_call(a):
    return pl.pallas_call(
        stage_kernel,
        in_specs=[pl.BlockSpec(memory_space=pl.ANY)],
        out_specs=vmem(),
        out_shape=jax.ShapeDtypeStruct(a.shape, a.dtype),
        scratch_shapes=[pltpu.SemaphoreType.DMA],
        compiler_params=kernel_params(16),
        cost_estimate=cost(0, 4 * a.size),
        name="stage",
    )(a)


def round_kernel(a_ref, out_ref):
    out_ref[...] = a_ref[0].T.astype(half)


def round_call(a):
    _, width, ranks = a.shape
    blk = width
    return pl.pallas_call(
        round_kernel,
        grid=(width // blk,),
        in_specs=[pl.BlockSpec((1, blk, ranks), lambda i: (0, i, 0))],
        out_specs=pl.BlockSpec((ranks, blk), lambda i: (0, i)),
        out_shape=jax.ShapeDtypeStruct((ranks, width), half),
        compiler_params=kernel_params(16),
        cost_estimate=cost(0, 6 * a.size),
        name="round_factors",
    )(a)


def compact_kernel(live_ref, b_ref, cot_ref, up_ref, first_ref, rest_ref, all_ref):
    up_ref[...] = b_ref[0].astype(half)
    blocks = live_ref.shape[0]
    blk_len = cot_ref.shape[0] // blocks
    starts, _ = starts_of(live_ref)
    all_ref[...] = jnp.zeros_like(all_ref)
    panels, _, lanes = all_ref.shape
    row = lax.broadcasted_iota(jnp.int32, (blk_len, lanes), 0)
    for b in range(blocks):
        for p in range(panels):
            piece = cot_ref[b * blk_len : (b + 1) * blk_len, p * lanes : (p + 1) * lanes].astype(wide)
            all_ref[p, pl.ds(starts[b], blk_len), :] = jnp.where(row < live_ref[b], piece, 0.0)
    room = first_ref.shape[0]
    for p in range(panels):
        cols = slice(p * lanes, (p + 1) * lanes)
        first_ref[:, cols] = all_ref[p, :room, :].astype(half)
        rest_ref[0, :, cols] = all_ref[p, room:, :].astype(half)


def compact_call(live, b, cot, room, copies):
    tok, kw = cot.shape
    shapes = [
        jax.ShapeDtypeStruct(b.shape[1:], half),
        jax.ShapeDtypeStruct((room, kw), half),
        jax.ShapeDtypeStruct((copies, tok - room, kw), half),
    ]
    specs = [resident(shapes[0]), resident(shapes[1]), pl.BlockSpec((1, tok - room, kw), lambda i: (0, 0, 0))]
    return pl.pallas_call(
        compact_kernel,
        grid=(1,),
        in_specs=[smem(), resident(b), resident(cot)],
        out_specs=specs,
        out_shape=shapes,
        scratch_shapes=[pltpu.VMEM((kw // min(kw, 128), tok, min(kw, 128)), wide)],
        compiler_params=kernel_params(56),
        cost_estimate=cost(0, 4 * tok * kw),
        name="compact",
    )(live, b, cot)


def ordered_kernel(z_ref, *refs):
    out_ref = refs[-1]
    own = refs[0].shape[0]
    for k, ref in enumerate(refs[:-1]):
        at = pl.multiple_of(jnp.bitwise_xor(z_ref[0], k) * own, own)
        out_ref[pl.ds(at, own), :] = ref[...]


def ordered_call(z, pieces):
    own, cols = pieces[0].shape
    n = len(pieces)
    if own % 16:
        return jnp.stack(pieces)[jnp.bitwise_xor(z[0], jnp.arange(n))].reshape(n * own, cols)
    return pl.pallas_call(
        ordered_kernel,
        in_specs=[smem()] + [vmem()] * n,
        out_specs=vmem(),
        out_shape=jax.ShapeDtypeStruct((n * own, cols), half),
        compiler_params=kernel_params(16),
        cost_estimate=cost(0, 4 * n * own * cols),
        name="ordered",
    )(z, *pieces)


def hidden_kernel(order, groups, d_ref, z_ref, live_ref, *refs):
    tables, x_ref, a_refs = refs[:3], refs[3], refs[4 : 4 + len(order)]
    out_refs, (all_ref, prod_ref, rows_ref, flat_ref) = refs[4 + len(order) : -4], refs[-4:]
    ranks = a_refs[0].shape[0]
    step = pl.program_id(0)

    @pl.when(step == 0)
    def _():
        for i, ref in enumerate(a_refs):
            all_ref[i * ranks : (i + 1) * ranks, :] = ref[...]

    blk = prod_ref.shape[0]
    prod_ref[...] = mm(x_ref[pl.ds(pl.multiple_of(step * blk, blk), blk), :], all_ref[...], NT)
    blocks = live_ref.shape[0]
    blk_len = rows_ref.shape[0] // blocks
    per_step = blk // blk_len
    first = step * per_step
    start = jnp.int32(0)
    for b in range(blocks):
        start = start + jnp.where(b < first, live_ref[b], 0)
    for b in range(per_step):
        near, _ = block_table(tables, first + b, d_ref[0])
        at = jnp.int32(0)
        for i, j in enumerate(order):
            at = jnp.where(near == j, i, at)
        cols = pl.ds(pl.multiple_of(at * ranks, ranks), ranks)
        rows_ref[pl.ds(start, blk_len), :] = prod_ref[b * blk_len : (b + 1) * blk_len, cols]
        start = start + live_ref[first + b]

    @pl.when(step == pl.num_programs(0) - 1)
    def _():
        flat_ref[...] = rows_ref[...].T
        own = ranks // groups
        for k, out_ref in enumerate(out_refs):
            at = pl.multiple_of(jnp.bitwise_xor(z_ref[0], k) * own, own)
            out_ref[...] = flat_ref[pl.ds(at, own), :].astype(half)


def hidden_call(d, z, live, tables, x, downs, order, groups):
    tok, width = x.shape
    ranks = downs[0].shape[0]
    blk = min(256, tok)
    own = ranks // groups
    shape = jax.ShapeDtypeStruct((own, tok), half)
    return pl.pallas_call(
        functools.partial(hidden_kernel, order, groups),
        grid=(tok // blk,),
        in_specs=[smem()] * 6
        + [vmem()]
        + [resident(a) for a in downs],
        out_specs=[resident(shape)] * groups,
        out_shape=[shape] * groups,
        scratch_shapes=[
            pltpu.VMEM((len(downs) * ranks, width), half),
            pltpu.VMEM((blk, len(downs) * ranks), wide),
            pltpu.VMEM((tok, ranks), wide),
            pltpu.VMEM((ranks, tok), wide),
        ],
        compiler_params=kernel_params(24),
        cost_estimate=cost(2 * tok * width * ranks * len(order), 2 * (x.size + 4 * downs[0].size)),
        name="hidden",
    )(d, z, live, *tables, x, *downs)


def upward_kernel(order, parts, d_ref, z_ref, live_ref, *refs):
    tables, cots, rest_ref = refs[:3], refs[3 : 3 + parts], refs[3 + parts]
    b_refs = refs[4 + parts : -5]
    full_ref, packed_ref, all_ref, acc_ref, rows_ref = refs[-5:]
    ranks = b_refs[0].shape[0]
    room, kw = cots[0].shape
    for i, ref in enumerate(b_refs):
        all_ref[i * ranks : (i + 1) * ranks, :] = ref[...]

    src = sources(z_ref[0], parts)

    def product(at, rows, pieces):
        acc = None
        for i, piece in enumerate(pieces):
            cols = pl.ds(pl.multiple_of(src[i] * kw, kw), kw)
            prod = mm(piece, all_ref[:, cols], NT)
            acc = prod if acc is None else acc + prod
        for i in range(len(order)):
            acc_ref[i, at : at + rows, :] = acc[:, i * ranks : (i + 1) * ranks]

    product(0, room, [ref[...] for ref in cots])
    starts, total = starts_of(live_ref)

    @pl.when(total > room)
    def _():
        product(room, rest_ref.shape[1], [rest_ref[i] for i in range(parts)])

    blocks = live_ref.shape[0]
    blk_len = full_ref.shape[0] // blocks
    rank_at = lax.broadcasted_iota(jnp.int32, (1, ranks), 1)
    row = lax.broadcasted_iota(jnp.int32, (blk_len, ranks), 0)
    for b in range(blocks):
        near, rank = block_table(tables, b, d_ref[0])
        scale = jnp.where(rank_at < rank, inverse_rank(rank, (1, ranks)), 0.0)
        for i, j in enumerate(order):
            cols = slice(i * ranks, (i + 1) * ranks)
            piece = acc_ref[i, pl.ds(starts[b], blk_len), :] * jnp.where(near == j, scale, 0.0)
            piece = jnp.where(row < live_ref[b], piece, 0.0)
            full_ref[b * blk_len : (b + 1) * blk_len, cols] = piece.astype(half)
            rows_ref[i, pl.ds(starts[b], blk_len), :] = piece
    for i in range(len(order)):
        packed_ref[:, i * ranks : (i + 1) * ranks] = rows_ref[i].astype(half)


def upward_call(d, z, live, tables, cots, rest, ups, order):
    ranks, value_width = ups[0].shape
    every = len(ups) * ranks
    tok = cots[0].shape[0] + rest.shape[1]
    shape = jax.ShapeDtypeStruct((tok, every), half)
    return pl.pallas_call(
        functools.partial(upward_kernel, order, len(cots)),
        in_specs=[smem()] * 6 + [vmem()] * (len(cots) + 1 + len(ups)),
        out_specs=[vmem()] * 2,
        out_shape=[shape, shape],
        scratch_shapes=[
            pltpu.VMEM((every, value_width), half),
            pltpu.VMEM((len(ups), tok, ranks), wide),
            pltpu.VMEM((len(ups), tok, ranks), wide),
        ],
        compiler_params=kernel_params(24),
        cost_estimate=cost(2 * tok * value_width * every, 2 * (tok * value_width + 2 * every * value_width)),
        name="upward",
    )(d, z, live, *tables, *cots, rest, *ups)


def down_kernel(ranks, start, x_ref, u_ref, keep_ref, send_ref):
    blk = keep_ref.shape[1]
    cols = pl.ds(pl.multiple_of(start + pl.program_id(0) * blk, blk), blk)
    acc = mm(x_ref[:, cols], u_ref[...], TN)
    per = keep_ref.shape[0]
    for i in range(per):
        keep_ref[i] = acc[:, i * ranks : (i + 1) * ranks].astype(half)
        send_ref[i] = acc[:, (per + i) * ranks : (per + i + 1) * ranks].astype(half)


def down_call(x, u, ranks, start, count):
    tok = x.shape[0]
    slots = u.shape[1] // ranks
    blk = min(512, count)
    shape = jax.ShapeDtypeStruct((slots // 2, count, ranks), half)
    return pl.pallas_call(
        functools.partial(down_kernel, ranks, start),
        grid=(count // blk,),
        in_specs=[vmem(), vmem()],
        out_specs=[pl.BlockSpec((slots // 2, blk, ranks), lambda i: (0, i, 0))] * 2,
        out_shape=[shape, shape],
        compiler_params=kernel_params(24),
        cost_estimate=cost(2 * tok * count * slots * ranks, 2 * (tok * count + slots * ranks * (tok + count))),
        name="down_grad",
    )(x, u)


def up_kernel(order, parts, n_hs, tail_rows, d_ref, z_ref, live_ref, *refs):
    tables, hs = refs[:3], refs[3 : 3 + n_hs]
    cots, rest_ref = refs[3 + n_hs : 3 + n_hs + parts], refs[3 + n_hs + parts]
    keep_ref, send_ref, acc_ref = refs[-3:]
    own, tok = hs[0].shape
    per = len(order) // 2
    blocks = live_ref.shape[0]
    total = hs[0][...].astype(wide)
    for h in hs[1:]:
        total = total + h[...].astype(wide)
    starts, live_rows = starts_of(live_ref)
    lane = lax.broadcasted_iota(jnp.int32, (1, tok), 1)
    slot = jnp.zeros((1, tok), jnp.int32)
    rank = jnp.ones((1, tok), jnp.int32)
    counts = [jnp.int32(0) for _ in order]
    for b in range(blocks):
        near, rank_b = block_table(tables, b, d_ref[0])
        slot = jnp.where(lane >= starts[b], near, slot)
        rank = jnp.where(lane >= starts[b], rank_b, rank)
        counts = [c + jnp.where(near == j, live_ref[b], 0) for c, j in zip(counts, order)]
    src = sources(z_ref[0], parts)
    rank_at = z_ref[0] * own + lax.broadcasted_iota(jnp.int32, total.shape, 0)
    scale = adapter_alpha_scale / rank.astype(wide)
    total = jnp.where((rank_at < rank) & (lane < live_rows), total * scale, 0.0)
    lhs = jnp.concatenate([jnp.where(slot == j, total, 0.0).astype(half) for j in order], axis=0)
    room, kw = cots[0].shape
    for i in range(parts):
        cols = pl.ds(pl.multiple_of(src[i] * kw, kw), kw)
        acc_ref[:, cols] = mm(lhs[:, :room], cots[i][...], NN)

    @pl.when(live_rows > room)
    def _():
        for i in range(parts):
            cols = pl.ds(pl.multiple_of(src[i] * kw, kw), kw)
            acc_ref[:, cols] = acc_ref[:, cols] + mm(lhs[:, room:], rest_ref[i], NN)

    row = lax.broadcasted_iota(jnp.int32, (tail_rows, keep_ref.shape[2]), 0)
    for k in range(per):
        for ref, at in ((keep_ref, k), (send_ref, per + k)):
            ref[k, :own, :] = acc_ref[at * own : (at + 1) * own, :].astype(half)
            tail = jnp.where(row == 0, counts[at] // 32, jnp.where(row == 1, counts[at] % 32, 0))
            ref[k, own:, :] = tail.astype(wide).astype(half)


def up_call(d, z, live, tables, hs, cots, rest, order, tail_rows=16):
    own, tok = hs[0].shape
    parts = len(cots)
    width = parts * cots[0].shape[1]
    shape = jax.ShapeDtypeStruct((len(order) // 2, own + tail_rows, width), half)
    return pl.pallas_call(
        functools.partial(up_kernel, order, parts, len(hs), tail_rows),
        in_specs=[smem()] * 6 + [vmem()] * (len(hs) + len(cots) + 1),
        out_specs=[vmem()] * 2,
        out_shape=[shape, shape],
        scratch_shapes=[pltpu.VMEM((len(order) * own, width), wide)],
        compiler_params=kernel_params(24),
        cost_estimate=cost(2 * len(order) * own * tok * width, 4 * tok * width),
        name="up_grad",
    )(d, z, live, *tables, *hs, *cots, rest)


def up_plain(d, z, live, tables, hs, cots, rest, order, tail_rows=16):
    tenant, slot_of, rank_of = tables
    own, tok = hs[0].shape
    room = tok - rest.shape[1]
    pick = tenant[:, None] == jnp.arange(slot_of.shape[0])[None, :]
    near = jnp.bitwise_xor(jnp.sum(jnp.where(pick, slot_of[None, :], 0), axis=1), d)
    rank = jnp.sum(jnp.where(pick, rank_of[None, :], 0), axis=1)
    ends = jnp.cumsum(live)
    lane = jnp.arange(tok, dtype=jnp.int32)[None, :]
    mine = (lane >= (ends - live)[:, None]) & (lane < ends[:, None])
    slot = jnp.sum(jnp.where(mine, near[:, None], 0), axis=0)[None, :]
    rank = jnp.maximum(jnp.sum(jnp.where(mine, rank[:, None], 0), axis=0), 1)[None, :]
    total = sum(h.astype(wide) for h in hs)
    rank_at = z * own + jnp.arange(own, dtype=jnp.int32)[:, None]
    total = total * (adapter_alpha_scale / rank.astype(wide))
    total = jnp.where((rank_at < rank) & (lane < ends[-1]), total, 0.0)
    lhs = jnp.concatenate([jnp.where(slot == j, total, 0).astype(half) for j in order], axis=0)
    cot = [jnp.concatenate(cots, axis=1)]
    cot.append(jnp.where(ends[-1] > room, jnp.concatenate(list(rest), axis=1), 0))
    cot = jnp.concatenate(cot, axis=0)
    grads = mm(lhs, cot, NN).astype(half).reshape(len(order), own, cot.shape[1])
    counts = jnp.sum(jnp.where(near[:, None] == jnp.array(order)[None, :], live[:, None], 0), axis=0)
    tail = jnp.pad(jnp.stack([counts // 32, counts % 32], axis=1), ((0, 0), (0, tail_rows - 2)))
    tail = jnp.broadcast_to(tail.astype(half)[:, :, None], (len(order), tail_rows, cot.shape[1]))
    both = jnp.concatenate([grads, tail], axis=1)
    return both[: len(order) // 2], both[len(order) // 2 :]


def base_kernel(parts, z_ref, live_ref, w_ref, *refs):
    cots, out_ref = refs[:-1], refs[-1]
    room, kw = cots[0].shape
    _, total = starts_of(live_ref)
    src = sources(z_ref[0], parts)
    blk = out_ref.shape[1] // pl.num_programs(0)
    cols = pl.ds(pl.multiple_of(pl.program_id(0) * blk, blk), blk)
    tile = min(256, room)
    for at in range(0, room, tile):

        @pl.when(at < total)
        def _(at=at):
            acc = None
            for i, cot in enumerate(cots):
                w = w_ref[cols, pl.ds(pl.multiple_of(src[i] * kw, kw), kw)]
                prod = mm(cot[at : at + tile, :], w, NT)
                acc = prod if acc is None else acc + prod
            out_ref[at : at + tile, cols] = acc


def base_call(z, live, w, cots, parts):
    room, kw = cots[0].shape
    width = w.shape[0]
    blk = min(512, width)
    return pl.pallas_call(
        functools.partial(base_kernel, parts),
        grid=(width // blk,),
        in_specs=[smem(), smem(), vmem()] + [vmem()] * len(cots),
        out_specs=vmem(),
        out_shape=jax.ShapeDtypeStruct((room, width), wide),
        compiler_params=kernel_params(16),
        cost_estimate=cost(2 * room * width * kw * len(cots), 4 * room * width),
        name="base",
    )(z, live, w, *cots)


def acts_kernel(parts, early, z_ref, live_ref, w_ref, u_ref, base_ref, rest_ref, *refs):
    cots, a_refs = refs[: parts - early], refs[parts - early : -3]
    out_ref, all_ref, acc_ref = refs[-3:]
    room, kw = cots[0].shape
    ranks = a_refs[0].shape[0]
    starts, total = starts_of(live_ref)
    src = sources(z_ref[0], parts)
    for i, ref in enumerate(a_refs):
        all_ref[i * ranks : (i + 1) * ranks, :] = ref[...]
    tok, blk = out_ref.shape
    cols = pl.ds(pl.multiple_of(pl.program_id(0) * blk, blk), blk)
    panels, _, lanes = acc_ref.shape

    def product(at, rows, acc, pieces):
        acc_u = mm(u_ref[at : at + rows, :], all_ref[...], NN)
        acc = acc_u if acc is None else acc + acc_u
        for i, piece in pieces:
            w = w_ref[cols, pl.ds(pl.multiple_of(src[i] * kw, kw), kw)]
            acc = acc + mm(piece, w, NT)
        for p in range(panels):
            acc_ref[p, at : at + rows, :] = acc[:, p * lanes : (p + 1) * lanes]

    tile = min(256, room)
    for at in range(0, room, tile):

        @pl.when(at < total)
        def _(at=at):
            first = base_ref[at : at + tile, cols] if early else None
            product(at, tile, first, [(early + i, cot[at : at + tile, :]) for i, cot in enumerate(cots)])

    @pl.when(total > room)
    def _():
        product(room, tok - room, None, [(i, rest_ref[i]) for i in range(parts)])

    blocks = live_ref.shape[0]
    blk_len = tok // blocks
    row = lax.broadcasted_iota(jnp.int32, (blk_len, lanes), 0)
    for b in range(blocks):
        for p in range(panels):
            piece = acc_ref[p, pl.ds(starts[b], blk_len), :]
            piece = jnp.where(row < live_ref[b], piece, 0.0)
            out_ref[b * blk_len : (b + 1) * blk_len, p * lanes : (p + 1) * lanes] = piece.astype(half)


def acts_call(z, live, w, u, base, cots, rest, downs):
    width, kfull = w.shape
    tok, every = u.shape
    ranks = downs[0].shape[0]
    blk = min(512, width)
    parts = rest.shape[0]
    return pl.pallas_call(
        functools.partial(acts_kernel, parts, parts - len(cots)),
        grid=(width // blk,),
        in_specs=[smem(), smem(), vmem(), vmem(), vmem(), vmem()]
        + [vmem()] * len(cots)
        + [pl.BlockSpec((ranks, blk), lambda i: (0, i))] * len(downs),
        out_specs=pl.BlockSpec((tok, blk), lambda i: (0, i)),
        out_shape=jax.ShapeDtypeStruct((tok, width), half),
        scratch_shapes=[
            pltpu.VMEM((every, blk), half),
            pltpu.VMEM((blk // 128, tok, 128), wide),
        ],
        compiler_params=kernel_params(24),
        cost_estimate=cost(2 * tok * width * (kfull + every), 2 * (w.size + every * width + tok * (width + kfull))),
        name="grad_acts",
    )(z, live, w, u, base, rest, *cots, *downs)


def together(*values):
    return lax.optimization_barrier(values)


def after(value, *others):
    return lax.optimization_barrier((value, *others))[0]


def shards(
    n_dp,
    n_tensor,
    activations,
    output_gradient,
    value_weight,
    adapter_down_factors,
    adapter_up_factors,
    down_first_moment,
    down_second_moment,
    up_first_moment,
    up_second_moment,
    block_tenant,
    block_live_tokens,
    tenant_storage_slot,
    tenant_adapter_rank,
):
    tok, width = activations.shape
    live = block_live_tokens
    slots = tenant_storage_slot.shape[0]
    assert adapter_down_factors.shape[0] == 1 and slots == n_dp
    ranks = adapter_down_factors.shape[2]
    own_ranks = adapter_up_factors.shape[1]
    kw = output_gradient.shape[1]
    z = lax.axis_index("tensor").astype(jnp.int32)
    d = lax.axis_index("dp").astype(jnp.int32)
    z_one, d_one = z[None], d[None]
    order = bit_order(slots)
    levels = [1 << b for b in range(slots.bit_length() - 1)]
    tables = (block_tenant, tenant_storage_slot, tenant_adapter_rank)
    ring = line_ring(n_tensor)
    ring_pairs = [(ring[i], ring[(i + 1) % n_tensor]) for i in range(n_tensor)]

    def onward(v):
        return lax.ppermute(v, "tensor", ring_pairs)

    room = tok * 3 // 4
    own_b, first, rest = compact_call(live, adapter_up_factors, output_gradient, room, n_tensor)

    def rest_of(v):
        out = [v[0]]
        for _ in range(n_tensor - 1):
            out.append(onward(out[-1]))
        return jnp.stack(out)

    cots = [first, onward(first)]
    ups = [own_b, swap(own_b, "tensor", n_tensor, 1)]
    own_a = round_call(after(adapter_down_factors, first))
    x = stage_call(after(activations, first))
    weight = stage_call(after(value_weight, first))

    cots[1], own_a, ups[1], x, weight = together(cots[1], own_a, ups[1], x, weight)
    cots.append(onward(cots[1]))
    bits = 2
    while bits < n_tensor:
        ups = ups + [swap(v, "tensor", n_tensor, bits) for v in ups]
        bits *= 2
    far = list(reversed(levels))
    downs = [own_a]
    for bits in far[:-1]:
        downs = downs + [swap(v, "dp", n_dp, bits) for v in downs]
    rest = lax.cond(jnp.sum(live) > room, rest_of, lambda v: v, after(rest, cots[1]))
    early = 2 if kw % 128 == 0 and n_tensor > 2 else 0
    base = base_call(z_one, live, weight, cots[:early], n_tensor) if early else jnp.zeros((8, 128), wide)

    cots[2], rest, base, *both = together(cots[2], rest, base, *downs, *ups)
    downs, ups = both[: len(downs)], both[len(downs) :]
    while len(cots) < n_tensor:
        cots.append(onward(cots[-1]))
    downs = downs + [swap(v, "dp", n_dp, far[-1]) for v in downs]
    ups = [ordered_call(z_one, ups)]
    for bits in far[:-1]:
        ups = ups + [swap(v, "dp", n_dp, bits) for v in ups]
    hs = list(hidden_call(d_one, z_one, live, tables, x, downs, order, n_tensor))

    hs = [hs[0]] + [swap(hs[k], "tensor", n_tensor, k) for k in range(1, n_tensor)]
    cots[-1], *both = together(cots[-1], *hs, *ups)
    hs, ups = both[: len(hs)], both[len(hs) :]
    ups = ups + [swap(v, "dp", n_dp, far[-1]) for v in ups]
    if kw % 128:
        at = jnp.array([ring.index(i) for i in range(n_tensor)], jnp.int32)
        away = (at[z] - at) % n_tensor
        in_order = lambda v: jnp.moveaxis(v[away], 0, 1).reshape(v.shape[1], n_tensor * kw)
        cots = [in_order(jnp.stack(cots))]
        rest = in_order(rest)[None]
    u, packed_u = upward_call(d_one, z_one, live, tables, cots, rest, ups, order)

    def other_sums(total, *others):
        for bits in levels[1:]:
            n = total.shape[0] // 2
            got = after(swap(total[n:].astype(half), "dp", n_dp, bits), *others)
            total = total[:n] + got.astype(wide)
        return total[0]

    rows = width // 2
    keep_0, send_0 = down_call(x, u, ranks, 0, rows)
    got_0 = swap(send_0, "dp", n_dp, 1)
    keep_1, send_1 = down_call(x, after(u, send_0), ranks, rows, rows)
    got_1 = swap(send_1, "dp", n_dp, 1)
    hs[0] = after(hs[0], send_1)
    if own_ranks % 16:
        keep_up, send_up = up_plain(d, z, live, tables, hs, cots, rest, order)
    else:
        keep_up, send_up = up_call(d_one, z_one, live, tables, hs, cots, rest, order)
    got_up = swap(send_up, "dp", n_dp, 1)
    down_0 = keep_0.astype(wide) + after(got_0, send_up).astype(wide)
    down_1 = keep_1.astype(wide) + after(got_1, down_0).astype(wide)
    up_sum = keep_up.astype(wide) + after(got_up, down_1).astype(wide)
    grad_acts = acts_call(
        z_one, live, weight, after(packed_u, down_1, up_sum), base, cots[early:], rest, downs
    )
    up_sum = other_sums(up_sum, grad_acts)
    denom = jnp.maximum(up_sum[own_ranks, 0] * 32.0 + up_sum[own_ranks + 1, 0], 1.0)

    up_grad = up_sum[None, :own_ranks] / denom
    new_up = moment_update_rule(adapter_up_factors, up_first_moment, up_second_moment, up_grad)
    down_sums = [other_sums(down_0, grad_acts), other_sums(down_1, grad_acts)]
    down_grad = jnp.concatenate(down_sums, axis=0)[None] / denom
    new_down = moment_update_rule(adapter_down_factors, down_first_moment, down_second_moment, down_grad)
    return (grad_acts, *new_down, *new_up)


def solution(mesh):
    tokens = P(("groups", "dp"), "tensor")
    factors = P(("groups", "dp"), "tensor", None)
    placed = (tokens, tokens, P("tensor", None), *([factors] * 6), P(("groups", "dp")), P(("groups", "dp")), P("groups"), P("groups"))
    return jax.shard_map(
        functools.partial(shards, mesh.shape["dp"], mesh.shape["tensor"]),
        mesh=mesh,
        in_specs=placed,
        out_specs=(tokens, *([factors] * 6)),
        check_vma=False,
    )
```

```python
import functools

import jax
import jax.numpy as jnp
from jax import lax
from jax.experimental import pallas as pl
from jax.experimental.pallas import tpu as pltpu
from jax.sharding import PartitionSpec as P

adapter_alpha_scale = 16.0
beta_one = 0.9
beta_two = 0.999
adam_eps = 1e-08
learn_rate = 0.001
adam_step = 10
half = jnp.bfloat16
wide = jnp.float32
MIB = 1 << 20
NT = (((1,), (1,)), ((), ()))
TN = (((0,), (0,)), ((), ()))
NN = (((1,), (0,)), ((), ()))


def mm(a, b, dims):
    return lax.dot_general(a, b, dims, preferred_element_type=wide)


def moment_update_rule(param, first, second, grad):
    new_first = beta_one * first + (1.0 - beta_one) * grad
    new_second = beta_two * second + (1.0 - beta_two) * grad * grad
    fixed_first = new_first / (1.0 - beta_one**adam_step)
    fixed_second = new_second / (1.0 - beta_two**adam_step)
    return (
        param - learn_rate * fixed_first / (jnp.sqrt(fixed_second) + adam_eps),
        new_first,
        new_second,
    )


def bit_order(n):
    if n == 1:
        return [0]
    inner = [2 * i for i in bit_order(n // 2)]
    return inner + [i + 1 for i in inner]


def paired(order):
    q = len(order) // 4
    return order[:q] + order[2 * q : 3 * q] + order[q : 2 * q] + order[3 * q :]


def line_ring(n):
    return [0] + list(range(1, n, 2)) + list(range(n - 2 + n % 2, 0, -2))


def swap(v, axis, n, bits):
    return lax.ppermute(v, axis, [(i, i ^ bits) for i in range(n)])


def kernel_params(mib):
    return pltpu.CompilerParams(vmem_limit_bytes=mib * MIB)


def cost(flops, nbytes):
    return pl.CostEstimate(flops=int(flops), bytes_accessed=int(nbytes), transcendentals=0)


def block_table(refs, b, d):
    tenant_ref, slot_ref, rank_ref = refs
    tenant = tenant_ref[b]
    return jnp.bitwise_xor(slot_ref[tenant], d), rank_ref[tenant]


def inverse_rank(rank, shape):
    return adapter_alpha_scale / jnp.full(shape, rank, jnp.int32).astype(wide)


def sources(z, n):
    ring = line_ring(n)
    out = []
    for i in range(n):
        came = [ring[(ring.index(k) - i) % n] for k in range(n)]
        at = came[0]
        for k in range(1, n):
            at = jnp.where(z == k, came[k], at)
        out.append(at)
    return out


def smem():
    return pl.BlockSpec(memory_space=pltpu.SMEM)


def resident(a):
    return pl.BlockSpec(a.shape, lambda *_, n=len(a.shape): (0,) * n)


def vmem():
    return pl.BlockSpec(memory_space=pltpu.VMEM)


def starts_of(live_ref):
    starts, at = [], 0
    for b in range(live_ref.shape[0]):
        starts.append(at)
        at = at + live_ref[b]
    return starts, at


def stage_kernel(from_ref, to_ref, sem):
    copy = pltpu.make_async_copy(from_ref, to_ref, sem)
    copy.start()
    copy.wait()


def stage_call(a):
    return pl.pallas_call(
        stage_kernel,
        in_specs=[pl.BlockSpec(memory_space=pl.ANY)],
        out_specs=vmem(),
        out_shape=jax.ShapeDtypeStruct(a.shape, a.dtype),
        scratch_shapes=[pltpu.SemaphoreType.DMA],
        compiler_params=kernel_params(16),
        cost_estimate=cost(0, 4 * a.size),
        name="stage",
    )(a)


def pack_kernel(live_ref, a_ref, b_ref, cot_ref, down_ref, up_ref, first_ref, rest_ref, all_ref):
    blocks = live_ref.shape[0]
    blk_len = cot_ref.shape[0] // blocks
    starts, _ = starts_of(live_ref)
    all_ref[...] = jnp.zeros_like(all_ref)
    panels, _, lanes = all_ref.shape
    row = lax.broadcasted_iota(jnp.int32, (blk_len, lanes), 0)
    for b in range(blocks):
        for p in range(panels):
            piece = cot_ref[b * blk_len : (b + 1) * blk_len, p * lanes : (p + 1) * lanes].astype(wide)
            all_ref[p, pl.ds(starts[b], blk_len), :] = jnp.where(row < live_ref[b], piece, 0.0)
    room = first_ref.shape[0]
    for p in range(panels):
        cols = slice(p * lanes, (p + 1) * lanes)
        first_ref[:, cols] = all_ref[p, :room, :].astype(half)
        rest_ref[0, :, cols] = all_ref[p, room:, :].astype(half)
    up_ref[...] = b_ref[0].astype(half)
    down_ref[...] = a_ref[0].T.astype(half)


def pack_call(live, a, b, cot, room, copies):
    tok, kw = cot.shape
    shapes = [
        jax.ShapeDtypeStruct((a.shape[2], a.shape[1]), half),
        jax.ShapeDtypeStruct(b.shape[1:], half),
        jax.ShapeDtypeStruct((room, kw), half),
        jax.ShapeDtypeStruct((copies, tok - room, kw), half),
    ]
    specs = [resident(v) for v in shapes[:-1]] + [pl.BlockSpec((1, tok - room, kw), lambda i: (0, 0, 0))]
    return pl.pallas_call(
        pack_kernel,
        grid=(1,),
        in_specs=[smem(), resident(a), resident(b), resident(cot)],
        out_specs=specs,
        out_shape=shapes,
        scratch_shapes=[pltpu.VMEM((kw // min(kw, 128), tok, min(kw, 128)), wide)],
        compiler_params=kernel_params(56),
        cost_estimate=cost(0, 4 * tok * kw + 6 * (a.size + b.size)),
        name="pack",
    )(live, a, b, cot)


def ordered_kernel(z_ref, live_ref, tenant_ref, slot_ref, *refs):
    out_ref = refs[-1]
    own = refs[0].shape[0]
    for k, ref in enumerate(refs[:-1]):
        at = pl.multiple_of(jnp.bitwise_xor(z_ref[0], k) * own, own)
        out_ref[pl.ds(at, own), :] = ref[...]
    ranks = own * (len(refs) - 1)
    shape = (out_ref.shape[0] - ranks, out_ref.shape[1])
    row, lane = lax.broadcasted_iota(jnp.int32, shape, 0), lax.broadcasted_iota(jnp.int32, shape, 1)
    tail = jnp.zeros(shape, jnp.int32)
    for q in range(slot_ref.shape[0]):
        count = jnp.int32(0)
        for b in range(live_ref.shape[0]):
            count = count + jnp.where(slot_ref[tenant_ref[b]] == q, live_ref[b], 0)
        digit = jnp.where(row == 0, count // 32, jnp.where(row == 1, count % 32, 0))
        tail = jnp.where(lane == q, digit, tail)
    out_ref[ranks:, :] = tail.astype(wide).astype(half)


def ordered_call(z, live, tables, pieces, tail_rows=16):
    own, cols = pieces[0].shape
    n = len(pieces)
    tenant, slot_of, _ = tables
    if own % 16:
        rows = jnp.stack(pieces)[jnp.bitwise_xor(z[0], jnp.arange(n))].reshape(n * own, cols)
        pick = tenant[:, None] == jnp.arange(slot_of.shape[0])[None, :]
        slot = jnp.sum(jnp.where(pick, slot_of[None, :], 0), axis=1)
        mine = slot[:, None] == jnp.arange(slot_of.shape[0])[None, :]
        counts = jnp.sum(jnp.where(mine, live[:, None], 0), axis=0)
        tail = jnp.stack([counts // 32, counts % 32]).astype(wide).astype(half)
        return jnp.concatenate([rows, jnp.pad(tail, ((0, tail_rows - 2), (0, cols - slot_of.shape[0])))], axis=0)
    return pl.pallas_call(
        ordered_kernel,
        in_specs=[smem()] * 4 + [vmem()] * n,
        out_specs=vmem(),
        out_shape=jax.ShapeDtypeStruct((n * own + tail_rows, cols), half),
        compiler_params=kernel_params(16),
        cost_estimate=cost(0, 4 * n * own * cols),
        name="ordered",
    )(z, live, tenant, slot_of, *pieces)


def hidden_kernel(order, groups, d_ref, z_ref, live_ref, *refs):
    tables, x_ref, a_refs, out_refs = refs[:3], refs[3], refs[4 : -4 - groups], refs[-4 - groups : -4]
    all_ref, prod_ref, rows_ref, flat_ref = refs[-4:]
    ranks = rows_ref.shape[1]
    step = pl.program_id(0)

    @pl.when(step == 0)
    def _():
        rows = a_refs[0].shape[0]
        for i, ref in enumerate(a_refs):
            all_ref[i * rows : (i + 1) * rows, :] = ref[...]

    blk = prod_ref.shape[0]
    prod_ref[...] = mm(x_ref[pl.ds(pl.multiple_of(step * blk, blk), blk), :], all_ref[...], NT)
    blocks = live_ref.shape[0]
    blk_len = rows_ref.shape[0] // blocks
    per_step = blk // blk_len
    first = step * per_step
    start = jnp.int32(0)
    for b in range(blocks):
        start = start + jnp.where(b < first, live_ref[b], 0)
    for b in range(per_step):
        near, _ = block_table(tables, first + b, d_ref[0])
        at = jnp.int32(0)
        for i, j in enumerate(order):
            at = jnp.where(near == j, i, at)
        cols = pl.ds(pl.multiple_of(at * ranks, ranks), ranks)
        rows_ref[pl.ds(start, blk_len), :] = prod_ref[b * blk_len : (b + 1) * blk_len, cols]
        start = start + live_ref[first + b]

    @pl.when(step == pl.num_programs(0) - 1)
    def _():
        flat_ref[...] = rows_ref[...].T
        own = ranks // groups
        for k, out_ref in enumerate(out_refs):
            at = pl.multiple_of(jnp.bitwise_xor(z_ref[0], k) * own, own)
            out_ref[...] = flat_ref[pl.ds(at, own), :].astype(half)


def hidden_call(d, z, live, tables, x, downs, order, groups):
    tok, width = x.shape
    every = sum(a.shape[0] for a in downs)
    ranks = every // len(order)
    blk = min(256, tok)
    own = ranks // groups
    shape = jax.ShapeDtypeStruct((own, tok), half)
    return pl.pallas_call(
        functools.partial(hidden_kernel, order, groups),
        grid=(tok // blk,),
        in_specs=[smem()] * 6
        + [vmem()]
        + [resident(a) for a in downs],
        out_specs=[resident(shape)] * groups,
        out_shape=[shape] * groups,
        scratch_shapes=[
            pltpu.VMEM((every, width), half),
            pltpu.VMEM((blk, every), wide),
            pltpu.VMEM((tok, ranks), wide),
            pltpu.VMEM((ranks, tok), wide),
        ],
        compiler_params=kernel_params(56),
        cost_estimate=cost(2 * tok * width * ranks * len(order), 2 * (x.size + 4 * downs[0].size)),
        name="hidden",
    )(d, z, live, *tables, x, *downs)


def upward_kernel(order, parts, d_ref, z_ref, live_ref, *refs):
    tables, cots, rest_ref = refs[:3], refs[3 : 3 + parts], refs[3 + parts]
    b_refs = refs[4 + parts : -6]
    full_ref, packed_ref, count_ref, all_ref, acc_ref, rows_ref = refs[-6:]
    ranks = acc_ref.shape[2]
    room, kw = cots[0].shape
    count = jnp.zeros((1, b_refs[0].shape[1]), wide)
    for i, ref in enumerate(b_refs):
        all_ref[i * ranks : (i + 1) * ranks, :] = ref[:ranks, :]
        tail = ref[ranks:, :].astype(wide)
        count = count + tail[0:1] * 32.0 + tail[1:2]
    lane = lax.broadcasted_iota(jnp.int32, count.shape, 1)
    count = jnp.sum(jnp.where(lane == d_ref[0], count, 0.0), axis=1, keepdims=True)
    count_ref[...] = jnp.broadcast_to(jnp.maximum(count, 1.0), count_ref.shape)

    src = sources(z_ref[0], parts)

    def product(at, rows, pieces):
        acc = None
        for i, piece in enumerate(pieces):
            cols = pl.ds(pl.multiple_of(src[i] * kw, kw), kw)
            prod = mm(piece, all_ref[:, cols], NT)
            acc = prod if acc is None else acc + prod
        for i in range(len(order)):
            acc_ref[i, at : at + rows, :] = acc[:, i * ranks : (i + 1) * ranks]

    product(0, room, [ref[...] for ref in cots])
    starts, total = starts_of(live_ref)

    @pl.when(total > room)
    def _():
        product(room, rest_ref.shape[1], [rest_ref[i] for i in range(parts)])

    blocks = live_ref.shape[0]
    blk_len = full_ref.shape[0] // blocks
    panels = paired(order)
    rank_at = lax.broadcasted_iota(jnp.int32, (1, ranks), 1)
    row = lax.broadcasted_iota(jnp.int32, (blk_len, ranks), 0)
    for b in range(blocks):
        near, rank = block_table(tables, b, d_ref[0])
        scale = jnp.where(rank_at < rank, inverse_rank(rank, (1, ranks)), 0.0)
        for i, j in enumerate(order):
            piece = acc_ref[i, pl.ds(starts[b], blk_len), :] * jnp.where(near == j, scale, 0.0)
            piece = jnp.where(row < live_ref[b], piece, 0.0)
            at = panels.index(j)
            full_ref[b * blk_len : (b + 1) * blk_len, at * ranks : (at + 1) * ranks] = piece.astype(half)
            rows_ref[i, pl.ds(starts[b], blk_len), :] = piece
    for i in range(len(order)):
        packed_ref[:, i * ranks : (i + 1) * ranks] = rows_ref[i].astype(half)


def upward_call(d, z, live, tables, cots, rest, ups, order, ranks):
    value_width = ups[0].shape[1]
    every = len(ups) * ranks
    tok = cots[0].shape[0] + rest.shape[1]
    shape = jax.ShapeDtypeStruct((tok, every), half)
    return pl.pallas_call(
        functools.partial(upward_kernel, order, len(cots)),
        in_specs=[smem()] * 6 + [vmem()] * (len(cots) + 1 + len(ups)),
        out_specs=[vmem()] * 3,
        out_shape=[shape, shape, jax.ShapeDtypeStruct((8, value_width), wide)],
        scratch_shapes=[
            pltpu.VMEM((every, value_width), half),
            pltpu.VMEM((len(ups), tok, ranks), wide),
            pltpu.VMEM((len(ups), tok, ranks), wide),
        ],
        compiler_params=kernel_params(24),
        cost_estimate=cost(2 * tok * value_width * every, 2 * (tok * value_width + 2 * every * value_width)),
        name="upward",
    )(d, z, live, *tables, *cots, rest, *ups)


def down_kernel(ranks, first, x_ref, u_ref, keep_ref, send_ref):
    count, blk, _ = keep_ref.shape
    x = x_ref[:, pl.ds(pl.multiple_of(pl.program_id(0) * blk, blk), blk)]
    acc = mm(x, u_ref[:, first * ranks : (first + 2 * count) * ranks], TN)
    for i in range(count):
        keep_ref[i] = acc[:, i * ranks : (i + 1) * ranks].astype(half)
        send_ref[i] = acc[:, (count + i) * ranks : (count + i + 1) * ranks].astype(half)


def down_call(x, u, ranks, first, count):
    tok, width = x.shape
    blk = min(512, width)
    shape = jax.ShapeDtypeStruct((count, width, ranks), half)
    return pl.pallas_call(
        functools.partial(down_kernel, ranks, first),
        grid=(width // blk,),
        in_specs=[vmem(), vmem()],
        out_specs=[pl.BlockSpec((count, blk, ranks), lambda i: (0, i, 0))] * 2,
        out_shape=[shape, shape],
        compiler_params=kernel_params(24),
        cost_estimate=cost(0, 4 * tok),
        name="down_grad",
    )(x, u)


def up_kernel(order, parts, n_hs, d_ref, z_ref, live_ref, *refs):
    tables, hs = refs[:3], refs[3 : 3 + n_hs]
    cots, rest_ref = refs[3 + n_hs : 3 + n_hs + parts], refs[3 + n_hs + parts]
    keep_ref, send_ref, acc_ref = refs[-3:]
    own, tok = hs[0].shape
    per = len(order) // 2
    blocks = live_ref.shape[0]
    total = hs[0][...].astype(wide)
    for h in hs[1:]:
        total = total + h[...].astype(wide)
    starts, live_rows = starts_of(live_ref)
    lane = lax.broadcasted_iota(jnp.int32, (1, tok), 1)
    slot = jnp.zeros((1, tok), jnp.int32)
    rank = jnp.ones((1, tok), jnp.int32)
    for b in range(blocks):
        near, rank_b = block_table(tables, b, d_ref[0])
        slot = jnp.where(lane >= starts[b], near, slot)
        rank = jnp.where(lane >= starts[b], rank_b, rank)
    src = sources(z_ref[0], parts)
    rank_at = z_ref[0] * own + lax.broadcasted_iota(jnp.int32, total.shape, 0)
    scale = adapter_alpha_scale / rank.astype(wide)
    total = jnp.where((rank_at < rank) & (lane < live_rows), total * scale, 0.0)
    lhs = jnp.concatenate([jnp.where(slot == j, total, 0.0).astype(half) for j in order], axis=0)
    room, kw = cots[0].shape
    for i in range(parts):
        cols = pl.ds(pl.multiple_of(src[i] * kw, kw), kw)
        acc_ref[:, cols] = mm(lhs[:, :room], cots[i][...], NN)

    @pl.when(live_rows > room)
    def _():
        for i in range(parts):
            cols = pl.ds(pl.multiple_of(src[i] * kw, kw), kw)
            acc_ref[:, cols] = acc_ref[:, cols] + mm(lhs[:, room:], rest_ref[i], NN)

    for k in range(per):
        for ref, at in ((keep_ref, k), (send_ref, per + k)):
            ref[k] = acc_ref[at * own : (at + 1) * own, :].astype(half)


def up_call(d, z, live, tables, hs, cots, rest, order):
    own, tok = hs[0].shape
    parts = len(cots)
    width = parts * cots[0].shape[1]
    shape = jax.ShapeDtypeStruct((len(order) // 2, own, width), half)
    return pl.pallas_call(
        functools.partial(up_kernel, order, parts, len(hs)),
        in_specs=[smem()] * 6 + [vmem()] * (len(hs) + len(cots) + 1),
        out_specs=[vmem()] * 2,
        out_shape=[shape, shape],
        scratch_shapes=[pltpu.VMEM((len(order) * own, width), wide)],
        compiler_params=kernel_params(24),
        cost_estimate=cost(2 * len(order) * own * tok * width, 4 * tok * width),
        name="up_grad",
    )(d, z, live, *tables, *hs, *cots, rest)


def up_plain(d, z, live, tables, hs, cots, rest, order):
    tenant, slot_of, rank_of = tables
    own, tok = hs[0].shape
    room = tok - rest.shape[1]
    pick = tenant[:, None] == jnp.arange(slot_of.shape[0])[None, :]
    near = jnp.bitwise_xor(jnp.sum(jnp.where(pick, slot_of[None, :], 0), axis=1), d)
    rank = jnp.sum(jnp.where(pick, rank_of[None, :], 0), axis=1)
    ends = jnp.cumsum(live)
    lane = jnp.arange(tok, dtype=jnp.int32)[None, :]
    mine = (lane >= (ends - live)[:, None]) & (lane < ends[:, None])
    slot = jnp.sum(jnp.where(mine, near[:, None], 0), axis=0)[None, :]
    rank = jnp.maximum(jnp.sum(jnp.where(mine, rank[:, None], 0), axis=0), 1)[None, :]
    total = sum(h.astype(wide) for h in hs)
    rank_at = z * own + jnp.arange(own, dtype=jnp.int32)[:, None]
    total = total * (adapter_alpha_scale / rank.astype(wide))
    total = jnp.where((rank_at < rank) & (lane < ends[-1]), total, 0.0)
    lhs = jnp.concatenate([jnp.where(slot == j, total, 0).astype(half) for j in order], axis=0)
    cot = [jnp.concatenate(cots, axis=1)]
    cot.append(jnp.where(ends[-1] > room, jnp.concatenate(list(rest), axis=1), 0))
    cot = jnp.concatenate(cot, axis=0)
    grads = mm(lhs, cot, NN).astype(half).reshape(len(order), own, cot.shape[1])
    return grads[: len(order) // 2], grads[len(order) // 2 :]


def base_kernel(parts, z_ref, live_ref, w_ref, *refs):
    cots, out_ref = refs[:-1], refs[-1]
    room, kw = cots[0].shape
    _, total = starts_of(live_ref)
    src = sources(z_ref[0], parts)
    blk = out_ref.shape[1] // pl.num_programs(0)
    cols = pl.ds(pl.multiple_of(pl.program_id(0) * blk, blk), blk)
    tile = min(256, room)
    for at in range(0, room, tile):

        @pl.when(at < total)
        def _(at=at):
            acc = None
            for i, cot in enumerate(cots):
                w = w_ref[cols, pl.ds(pl.multiple_of(src[i] * kw, kw), kw)]
                prod = mm(cot[at : at + tile, :], w, NT)
                acc = prod if acc is None else acc + prod
            out_ref[at : at + tile, cols] = acc


def base_call(z, live, w, cots, parts):
    room, kw = cots[0].shape
    width = w.shape[0]
    blk = min(512, width)
    return pl.pallas_call(
        functools.partial(base_kernel, parts),
        grid=(width // blk,),
        in_specs=[smem(), smem(), vmem()] + [vmem()] * len(cots),
        out_specs=vmem(),
        out_shape=jax.ShapeDtypeStruct((room, width), wide),
        compiler_params=kernel_params(16),
        cost_estimate=cost(2 * room * width * kw * len(cots), 4 * room * width),
        name="base",
    )(z, live, w, *cots)


def acts_kernel(parts, early, z_ref, live_ref, w_ref, u_ref, base_ref, rest_ref, *refs):
    cots, a_refs = refs[: parts - early], refs[parts - early : -3]
    out_ref, all_ref, acc_ref = refs[-3:]
    room, kw = cots[0].shape
    ranks = a_refs[0].shape[0]
    starts, total = starts_of(live_ref)
    src = sources(z_ref[0], parts)
    for i, ref in enumerate(a_refs):
        all_ref[i * ranks : (i + 1) * ranks, :] = ref[...]
    tok, blk = out_ref.shape
    cols = pl.ds(pl.multiple_of(pl.program_id(0) * blk, blk), blk)
    panels, _, lanes = acc_ref.shape

    def product(at, rows, acc, pieces):
        acc_u = mm(u_ref[at : at + rows, :], all_ref[...], NN)
        acc = acc_u if acc is None else acc + acc_u
        for i, piece in pieces:
            w = w_ref[cols, pl.ds(pl.multiple_of(src[i] * kw, kw), kw)]
            acc = acc + mm(piece, w, NT)
        for p in range(panels):
            acc_ref[p, at : at + rows, :] = acc[:, p * lanes : (p + 1) * lanes]

    tile = min(256, room)
    for at in range(0, room, tile):

        @pl.when(at < total)
        def _(at=at):
            first = base_ref[at : at + tile, cols] if early else None
            product(at, tile, first, [(early + i, cot[at : at + tile, :]) for i, cot in enumerate(cots)])

    @pl.when(total > room)
    def _():
        product(room, tok - room, None, [(i, rest_ref[i]) for i in range(parts)])

    blocks = live_ref.shape[0]
    blk_len = tok // blocks
    row = lax.broadcasted_iota(jnp.int32, (blk_len, lanes), 0)
    for b in range(blocks):
        for p in range(panels):
            piece = acc_ref[p, pl.ds(starts[b], blk_len), :]
            piece = jnp.where(row < live_ref[b], piece, 0.0)
            out_ref[b * blk_len : (b + 1) * blk_len, p * lanes : (p + 1) * lanes] = piece.astype(half)


def acts_call(z, live, w, u, base, cots, rest, downs):
    width, kfull = w.shape
    tok, every = u.shape
    ranks = downs[0].shape[0]
    blk = min(512, width)
    parts = rest.shape[0]
    return pl.pallas_call(
        functools.partial(acts_kernel, parts, parts - len(cots)),
        grid=(width // blk,),
        in_specs=[smem(), smem(), vmem(), vmem(), vmem(), vmem()]
        + [vmem()] * len(cots)
        + [pl.BlockSpec((ranks, blk), lambda i: (0, i))] * len(downs),
        out_specs=pl.BlockSpec((tok, blk), lambda i: (0, i)),
        out_shape=jax.ShapeDtypeStruct((tok, width), half),
        scratch_shapes=[
            pltpu.VMEM((every, blk), half),
            pltpu.VMEM((blk // 128, tok, 128), wide),
        ],
        compiler_params=kernel_params(24),
        cost_estimate=cost(0, 4 * tok),
        name="grad_acts",
    )(z, live, w, u, base, rest, *cots, *downs)


def together(*values):
    return lax.optimization_barrier(values)


def after(value, *others):
    return lax.optimization_barrier((value, *others))[0]


def shards(
    n_dp,
    n_tensor,
    activations,
    output_gradient,
    value_weight,
    adapter_down_factors,
    adapter_up_factors,
    down_first_moment,
    down_second_moment,
    up_first_moment,
    up_second_moment,
    block_tenant,
    block_live_tokens,
    tenant_storage_slot,
    tenant_adapter_rank,
):
    tok, width = activations.shape
    live = block_live_tokens
    slots = tenant_storage_slot.shape[0]
    assert adapter_down_factors.shape[0] == 1 and slots == n_dp and n_dp >= 4
    ranks = adapter_down_factors.shape[2]
    own_ranks = adapter_up_factors.shape[1]
    kw = output_gradient.shape[1]
    z = lax.axis_index("tensor").astype(jnp.int32)
    d = lax.axis_index("dp").astype(jnp.int32)
    z_one, d_one = z[None], d[None]
    order = bit_order(slots)
    levels = [1 << b for b in range(slots.bit_length() - 1)]
    tables = (block_tenant, tenant_storage_slot, tenant_adapter_rank)
    ring = line_ring(n_tensor)
    ring_pairs = [(ring[i], ring[(i + 1) % n_tensor]) for i in range(n_tensor)]

    def onward(v):
        return lax.ppermute(v, "tensor", ring_pairs)

    room = tok * 3 // 4
    own_a, own_b, first, rest = pack_call(
        live, adapter_down_factors, adapter_up_factors, output_gradient, room, n_tensor
    )

    def rest_of(v):
        out = [v[0]]
        for _ in range(n_tensor - 1):
            out.append(onward(out[-1]))
        return jnp.stack(out)

    cots = [first, onward(first)]
    ups = [own_b, swap(own_b, "tensor", n_tensor, 1)]
    far = list(reversed(levels))
    downs = [own_a]
    for bits in far[:-1]:
        downs = downs + [swap(v, "dp", n_dp, bits) for v in downs]

    rest = lax.cond(jnp.sum(live) > room, rest_of, lambda v: v, rest)

    cots[1], rest, *ups = together(cots[1], rest, *ups)
    cots.append(onward(cots[1]))
    bits = 2
    while bits < n_tensor:
        ups = ups + [swap(v, "tensor", n_tensor, bits) for v in ups]
        bits *= 2
    downs = [after(v, cots[1]) for v in downs]
    downs = downs + [swap(v, "dp", n_dp, far[-1]) for v in downs]
    hs = list(hidden_call(d_one, z_one, live, tables, activations, downs, order, n_tensor))

    cots[2], *both = together(cots[2], *hs, *ups)
    hs, ups = both[: len(hs)], both[len(hs) :]
    while len(cots) < n_tensor:
        cots.append(onward(cots[-1]))
    ups = [ordered_call(z_one, live, tables, ups)]
    for bits in far[:-1]:
        ups = ups + [swap(v, "dp", n_dp, bits) for v in ups]
    hs = [hs[0]] + [swap(hs[k], "tensor", n_tensor, k) for k in range(1, n_tensor)]
    early = 3 if kw % 128 == 0 and n_tensor > 3 else 0
    base = jnp.zeros((8, 128), wide)
    if early:
        base = base_call(z_one, live, value_weight, cots[:early], n_tensor)
    cots[-1], base, *both = together(cots[-1], base, *hs, *ups)
    hs, ups = both[: len(hs)], both[len(hs) :]
    ups = ups + [swap(v, "dp", n_dp, far[-1]) for v in ups]
    if kw % 128:
        at = jnp.array([ring.index(i) for i in range(n_tensor)], jnp.int32)
        away = (at[z] - at) % n_tensor
        in_order = lambda v: jnp.moveaxis(v[away], 0, 1).reshape(v.shape[1], n_tensor * kw)
        cots = [in_order(jnp.stack(cots))]
        rest = in_order(rest)[None]
    def other_sums(total, levels, *others):
        for bits in levels:
            n = total.shape[0] // 2
            got = after(swap(total[n:].astype(half), "dp", n_dp, bits), *others)
            total = total[:n] + got.astype(wide)
        return total[0]

    if own_ranks % 16:
        keep_up, send_up = up_plain(d, z, live, tables, hs, cots, rest, order)
    else:
        keep_up, send_up = up_call(d_one, z_one, live, tables, hs, cots, rest, order)
    got_up = swap(send_up, "dp", n_dp, 1)
    u, packed_u, count = upward_call(d_one, z_one, live, tables, cots, after(rest, send_up), ups, order, ranks)
    quarter = slots // 4
    keep_far, send_far = down_call(activations, u, ranks, 2 * quarter, quarter)
    got_far = swap(send_far, "dp", n_dp, 1)
    keep_near, send_near = down_call(activations, after(u, send_far), ranks, 0, quarter)
    sum_far = (keep_far.astype(wide) + after(got_far, send_near).astype(wide)).astype(half)
    got_far = swap(sum_far, "dp", n_dp, levels[1])
    got_near = swap(send_near, "dp", n_dp, 1)
    up_sum = keep_up.astype(wide) + after(got_up, sum_far).astype(wide)
    got_near = after(got_near, up_sum)
    grad_acts = acts_call(z_one, live, value_weight, after(packed_u, got_near), base, cots[early:], rest, downs)
    down_sum = keep_near.astype(wide) + got_near.astype(wide) + after(got_far, grad_acts).astype(wide)
    down_grad = other_sums(down_sum, levels[2:])[None] / count[None, :1, :ranks]
    new_down = moment_update_rule(adapter_down_factors, down_first_moment, down_second_moment, down_grad)
    up_grad = other_sums(up_sum, levels[1:], new_down[0])[None] / count[None, :1, :]
    new_up = moment_update_rule(adapter_up_factors, up_first_moment, up_second_moment, up_grad)
    return (grad_acts, *new_down, *new_up)


def solution(mesh):
    tokens = P(("groups", "dp"), "tensor")
    factors = P(("groups", "dp"), "tensor", None)
    placed = (tokens, tokens, P("tensor", None), *([factors] * 6), P(("groups", "dp")), P(("groups", "dp")), P("groups"), P("groups"))
    return jax.shard_map(
        functools.partial(shards, mesh.shape["dp"], mesh.shape["tensor"]),
        mesh=mesh,
        in_specs=placed,
        out_specs=(tokens, *([factors] * 6)),
        check_vma=False,
    )
```

```python
import functools

import jax
import jax.numpy as jnp
from jax import lax
from jax.experimental import pallas as pl
from jax.experimental.pallas import tpu as pltpu
from jax.sharding import PartitionSpec as P

adapter_alpha_scale = 16.0
beta_one = 0.9
beta_two = 0.999
adam_eps = 1e-08
learn_rate = 0.001
adam_step = 10
half = jnp.bfloat16
wide = jnp.float32
MIB = 1 << 20
NT = (((1,), (1,)), ((), ()))
TN = (((0,), (0,)), ((), ()))
NN = (((1,), (0,)), ((), ()))


def mm(a, b, dims):
    return lax.dot_general(a, b, dims, preferred_element_type=wide)


def moment_update_rule(param, first, second, grad):
    new_first = beta_one * first + (1.0 - beta_one) * grad
    new_second = beta_two * second + (1.0 - beta_two) * grad * grad
    fixed_first = new_first / (1.0 - beta_one**adam_step)
    fixed_second = new_second / (1.0 - beta_two**adam_step)
    return (
        param - learn_rate * fixed_first / (jnp.sqrt(fixed_second) + adam_eps),
        new_first,
        new_second,
    )


def bit_order(n):
    if n == 1:
        return [0]
    inner = [2 * i for i in bit_order(n // 2)]
    return inner + [i + 1 for i in inner]


def paired(order):
    q = len(order) // 4
    return order[:q] + order[2 * q : 3 * q] + order[q : 2 * q] + order[3 * q :]


def line_ring(n):
    return [0] + list(range(1, n, 2)) + list(range(n - 2 + n % 2, 0, -2))


def swap(v, axis, n, bits):
    return lax.ppermute(v, axis, [(i, i ^ bits) for i in range(n)])


def kernel_params(mib):
    return pltpu.CompilerParams(vmem_limit_bytes=mib * MIB)


def cost(flops, nbytes):
    return pl.CostEstimate(flops=int(flops), bytes_accessed=int(nbytes), transcendentals=0)


def block_table(refs, b, d):
    tenant_ref, slot_ref, rank_ref = refs
    tenant = tenant_ref[b]
    return jnp.bitwise_xor(slot_ref[tenant], d), rank_ref[tenant]


def inverse_rank(rank, shape):
    return adapter_alpha_scale / jnp.full(shape, rank, jnp.int32).astype(wide)


def sources(z, n):
    ring = line_ring(n)
    out = []
    for i in range(n):
        came = [ring[(ring.index(k) - i) % n] for k in range(n)]
        at = came[0]
        for k in range(1, n):
            at = jnp.where(z == k, came[k], at)
        out.append(at)
    return out


def smem():
    return pl.BlockSpec(memory_space=pltpu.SMEM)


def resident(a):
    return pl.BlockSpec(a.shape, lambda *_, n=len(a.shape): (0,) * n)


def vmem():
    return pl.BlockSpec(memory_space=pltpu.VMEM)


def starts_of(live_ref):
    starts, at = [], 0
    for b in range(live_ref.shape[0]):
        starts.append(at)
        at = at + live_ref[b]
    return starts, at


def stage_kernel(from_ref, to_ref, sem):
    copy = pltpu.make_async_copy(from_ref, to_ref, sem)
    copy.start()
    copy.wait()


def stage_call(a):
    return pl.pallas_call(
        stage_kernel,
        in_specs=[pl.BlockSpec(memory_space=pl.ANY)],
        out_specs=vmem(),
        out_shape=jax.ShapeDtypeStruct(a.shape, a.dtype),
        scratch_shapes=[pltpu.SemaphoreType.DMA],
        compiler_params=kernel_params(16),
        cost_estimate=cost(0, 4 * a.size),
        name="stage",
    )(a)


def round_kernel(a_ref, low_ref, high_ref):
    turned = a_ref[0].T.astype(half)
    low_ref[...] = turned[: low_ref.shape[0]]
    high_ref[...] = turned[low_ref.shape[0] :]


def round_call(a):
    _, width, ranks = a.shape
    blk = width
    return pl.pallas_call(
        round_kernel,
        grid=(width // blk,),
        in_specs=[pl.BlockSpec((1, blk, ranks), lambda i: (0, i, 0))],
        out_specs=[pl.BlockSpec((ranks // 2, blk), lambda i: (0, i))] * 2,
        out_shape=[jax.ShapeDtypeStruct((ranks // 2, width), half)] * 2,
        compiler_params=kernel_params(16),
        cost_estimate=cost(0, 6 * a.size),
        name="round_factors",
    )(a)


def pack_kernel(live_ref, b_ref, cot_ref, up_ref, first_ref, rest_ref, all_ref):
    blocks = live_ref.shape[0]
    blk_len = cot_ref.shape[0] // blocks
    starts, _ = starts_of(live_ref)
    all_ref[...] = jnp.zeros_like(all_ref)
    panels, _, lanes = all_ref.shape
    row = lax.broadcasted_iota(jnp.int32, (blk_len, lanes), 0)
    for b in range(blocks):
        for p in range(panels):
            piece = cot_ref[b * blk_len : (b + 1) * blk_len, p * lanes : (p + 1) * lanes].astype(wide)
            all_ref[p, pl.ds(starts[b], blk_len), :] = jnp.where(row < live_ref[b], piece, 0.0)
    room = first_ref.shape[0]
    for p in range(panels):
        cols = slice(p * lanes, (p + 1) * lanes)
        first_ref[:, cols] = all_ref[p, :room, :].astype(half)
        rest_ref[0, :, cols] = all_ref[p, room:, :].astype(half)
    up_ref[...] = b_ref[0].astype(half)


def pack_call(live, b, cot, room, copies):
    tok, kw = cot.shape
    shapes = [
        jax.ShapeDtypeStruct(b.shape[1:], half),
        jax.ShapeDtypeStruct((room, kw), half),
        jax.ShapeDtypeStruct((copies, tok - room, kw), half),
    ]
    specs = [resident(v) for v in shapes[:-1]] + [pl.BlockSpec((1, tok - room, kw), lambda i: (0, 0, 0))]
    return pl.pallas_call(
        pack_kernel,
        grid=(1,),
        in_specs=[smem(), resident(b), resident(cot)],
        out_specs=specs,
        out_shape=shapes,
        scratch_shapes=[pltpu.VMEM((kw // min(kw, 128), tok, min(kw, 128)), wide)],
        compiler_params=kernel_params(56),
        cost_estimate=cost(0, 4 * tok * kw + 6 * b.size),
        name="pack",
    )(live, b, cot)


def ordered_kernel(z_ref, live_ref, tenant_ref, slot_ref, *refs):
    out_ref = refs[-1]
    own = refs[0].shape[0]
    for k, ref in enumerate(refs[:-1]):
        at = pl.multiple_of(jnp.bitwise_xor(z_ref[0], k) * own, own)
        out_ref[pl.ds(at, own), :] = ref[...]
    ranks = own * (len(refs) - 1)
    shape = (out_ref.shape[0] - ranks, out_ref.shape[1])
    row, lane = lax.broadcasted_iota(jnp.int32, shape, 0), lax.broadcasted_iota(jnp.int32, shape, 1)
    tail = jnp.zeros(shape, jnp.int32)
    for q in range(slot_ref.shape[0]):
        count = jnp.int32(0)
        for b in range(live_ref.shape[0]):
            count = count + jnp.where(slot_ref[tenant_ref[b]] == q, live_ref[b], 0)
        digit = jnp.where(row == 0, count // 32, jnp.where(row == 1, count % 32, 0))
        tail = jnp.where(lane == q, digit, tail)
    out_ref[ranks:, :] = tail.astype(wide).astype(half)


def ordered_call(z, live, tables, pieces, tail_rows=16):
    own, cols = pieces[0].shape
    n = len(pieces)
    tenant, slot_of, _ = tables
    if own % 16:
        rows = jnp.stack(pieces)[jnp.bitwise_xor(z[0], jnp.arange(n))].reshape(n * own, cols)
        pick = tenant[:, None] == jnp.arange(slot_of.shape[0])[None, :]
        slot = jnp.sum(jnp.where(pick, slot_of[None, :], 0), axis=1)
        mine = slot[:, None] == jnp.arange(slot_of.shape[0])[None, :]
        counts = jnp.sum(jnp.where(mine, live[:, None], 0), axis=0)
        tail = jnp.stack([counts // 32, counts % 32]).astype(wide).astype(half)
        return jnp.concatenate([rows, jnp.pad(tail, ((0, tail_rows - 2), (0, cols - slot_of.shape[0])))], axis=0)
    return pl.pallas_call(
        ordered_kernel,
        in_specs=[smem()] * 4 + [vmem()] * n,
        out_specs=vmem(),
        out_shape=jax.ShapeDtypeStruct((n * own + tail_rows, cols), half),
        compiler_params=kernel_params(16),
        cost_estimate=cost(0, 4 * n * own * cols),
        name="ordered",
    )(z, live, tenant, slot_of, *pieces)


def hidden_kernel(order, groups, d_ref, z_ref, live_ref, *refs):
    tables, x_ref, a_refs, out_refs = refs[:3], refs[3], refs[4 : -4 - groups], refs[-4 - groups : -4]
    all_ref, prod_ref, rows_ref, flat_ref = refs[-4:]
    ranks = rows_ref.shape[1]
    step = pl.program_id(0)

    @pl.when(step == 0)
    def _():
        rows = a_refs[0].shape[0]
        for i, ref in enumerate(a_refs):
            all_ref[i * rows : (i + 1) * rows, :] = ref[...]

    blk = prod_ref.shape[0]
    prod_ref[...] = mm(x_ref[pl.ds(pl.multiple_of(step * blk, blk), blk), :], all_ref[...], NT)
    blocks = live_ref.shape[0]
    blk_len = rows_ref.shape[0] // blocks
    per_step = blk // blk_len
    first = step * per_step
    start = jnp.int32(0)
    for b in range(blocks):
        start = start + jnp.where(b < first, live_ref[b], 0)
    for b in range(per_step):
        near, _ = block_table(tables, first + b, d_ref[0])
        at = jnp.int32(0)
        for i, j in enumerate(order):
            at = jnp.where(near == j, i, at)
        cols = pl.ds(pl.multiple_of(at * ranks, ranks), ranks)
        rows_ref[pl.ds(start, blk_len), :] = prod_ref[b * blk_len : (b + 1) * blk_len, cols]
        start = start + live_ref[first + b]

    @pl.when(step == pl.num_programs(0) - 1)
    def _():
        flat_ref[...] = rows_ref[...].T
        own = ranks // groups
        for k, out_ref in enumerate(out_refs):
            at = pl.multiple_of(jnp.bitwise_xor(z_ref[0], k) * own, own)
            out_ref[...] = flat_ref[pl.ds(at, own), :].astype(half)


def hidden_call(d, z, live, tables, x, downs, order, groups):
    tok, width = x.shape
    every = sum(a.shape[0] for a in downs)
    ranks = every // len(order)
    blk = min(256, tok)
    own = ranks // groups
    shape = jax.ShapeDtypeStruct((own, tok), half)
    return pl.pallas_call(
        functools.partial(hidden_kernel, order, groups),
        grid=(tok // blk,),
        in_specs=[smem()] * 6
        + [vmem()] * (1 + len(downs)),
        out_specs=[resident(shape)] * groups,
        out_shape=[shape] * groups,
        scratch_shapes=[
            pltpu.VMEM((every, width), half),
            pltpu.VMEM((blk, every), wide),
            pltpu.VMEM((tok, ranks), wide),
            pltpu.VMEM((ranks, tok), wide),
        ],
        compiler_params=kernel_params(24),
        cost_estimate=cost(0, 4 * tok),
        name="hidden",
    )(d, z, live, *tables, x, *downs)


def upward_kernel(order, parts, d_ref, z_ref, live_ref, *refs):
    tables, cots, rest_ref = refs[:3], refs[3 : 3 + parts], refs[3 + parts]
    b_refs = refs[4 + parts : -6]
    full_ref, packed_ref, count_ref, all_ref, acc_ref, rows_ref = refs[-6:]
    ranks = acc_ref.shape[2]
    room, kw = cots[0].shape
    count = jnp.zeros((1, b_refs[0].shape[1]), wide)
    for i, ref in enumerate(b_refs):
        all_ref[i * ranks : (i + 1) * ranks, :] = ref[:ranks, :]
        tail = ref[ranks:, :].astype(wide)
        count = count + tail[0:1] * 32.0 + tail[1:2]
    lane = lax.broadcasted_iota(jnp.int32, count.shape, 1)
    count = jnp.sum(jnp.where(lane == d_ref[0], count, 0.0), axis=1, keepdims=True)
    count_ref[...] = jnp.broadcast_to(jnp.maximum(count, 1.0), count_ref.shape)

    src = sources(z_ref[0], parts)

    def product(at, rows, pieces):
        acc = None
        for i, piece in enumerate(pieces):
            cols = pl.ds(pl.multiple_of(src[i] * kw, kw), kw)
            prod = mm(piece, all_ref[:, cols], NT)
            acc = prod if acc is None else acc + prod
        for i in range(len(order)):
            acc_ref[i, at : at + rows, :] = acc[:, i * ranks : (i + 1) * ranks]

    product(0, room, [ref[...] for ref in cots])
    starts, total = starts_of(live_ref)

    @pl.when(total > room)
    def _():
        product(room, rest_ref.shape[1], [rest_ref[i] for i in range(parts)])

    blocks = live_ref.shape[0]
    blk_len = full_ref.shape[0] // blocks
    panels = paired(order)
    rank_at = lax.broadcasted_iota(jnp.int32, (1, ranks), 1)
    row = lax.broadcasted_iota(jnp.int32, (blk_len, ranks), 0)
    for b in range(blocks):
        near, rank = block_table(tables, b, d_ref[0])
        scale = jnp.where(rank_at < rank, inverse_rank(rank, (1, ranks)), 0.0)
        for i, j in enumerate(order):
            piece = acc_ref[i, pl.ds(starts[b], blk_len), :] * jnp.where(near == j, scale, 0.0)
            piece = jnp.where(row < live_ref[b], piece, 0.0)
            at = panels.index(j)
            full_ref[b * blk_len : (b + 1) * blk_len, at * ranks : (at + 1) * ranks] = piece.astype(half)
            rows_ref[i, pl.ds(starts[b], blk_len), :] = piece
    for i in range(len(order)):
        packed_ref[:, i * ranks : (i + 1) * ranks] = rows_ref[i].astype(half)


def upward_call(d, z, live, tables, cots, rest, ups, order, ranks):
    value_width = ups[0].shape[1]
    every = len(ups) * ranks
    tok = cots[0].shape[0] + rest.shape[1]
    shape = jax.ShapeDtypeStruct((tok, every), half)
    return pl.pallas_call(
        functools.partial(upward_kernel, order, len(cots)),
        in_specs=[smem()] * 6 + [vmem()] * (len(cots) + 1 + len(ups)),
        out_specs=[vmem()] * 3,
        out_shape=[shape, shape, jax.ShapeDtypeStruct((8, value_width), wide)],
        scratch_shapes=[
            pltpu.VMEM((every, value_width), half),
            pltpu.VMEM((len(ups), tok, ranks), wide),
            pltpu.VMEM((len(ups), tok, ranks), wide),
        ],
        compiler_params=kernel_params(24),
        cost_estimate=cost(2 * tok * value_width * every, 2 * (tok * value_width + 2 * every * value_width)),
        name="upward",
    )(d, z, live, *tables, *cots, rest, *ups)


def down_kernel(ranks, first, x_ref, u_ref, keep_ref, send_ref):
    count, blk, _ = keep_ref.shape
    x = x_ref[:, pl.ds(pl.multiple_of(pl.program_id(0) * blk, blk), blk)]
    acc = mm(x, u_ref[:, first * ranks : (first + 2 * count) * ranks], TN)
    for i in range(count):
        keep_ref[i] = acc[:, i * ranks : (i + 1) * ranks].astype(half)
        send_ref[i] = acc[:, (count + i) * ranks : (count + i + 1) * ranks].astype(half)


def down_call(x, u, ranks, first, count):
    tok, width = x.shape
    blk = min(512, width)
    shape = jax.ShapeDtypeStruct((count, width, ranks), half)
    return pl.pallas_call(
        functools.partial(down_kernel, ranks, first),
        grid=(width // blk,),
        in_specs=[vmem(), vmem()],
        out_specs=[pl.BlockSpec((count, blk, ranks), lambda i: (0, i, 0))] * 2,
        out_shape=[shape, shape],
        compiler_params=kernel_params(24),
        cost_estimate=cost(0, 4 * tok),
        name="down_grad",
    )(x, u)


def up_kernel(order, parts, n_hs, d_ref, z_ref, live_ref, *refs):
    tables, hs = refs[:3], refs[3 : 3 + n_hs]
    cots, rest_ref = refs[3 + n_hs : 3 + n_hs + parts], refs[3 + n_hs + parts]
    keep_ref, send_ref, acc_ref = refs[-3:]
    own, tok = hs[0].shape
    per = len(order) // 2
    blocks = live_ref.shape[0]
    total = hs[0][...].astype(wide)
    for h in hs[1:]:
        total = total + h[...].astype(wide)
    starts, live_rows = starts_of(live_ref)
    lane = lax.broadcasted_iota(jnp.int32, (1, tok), 1)
    slot = jnp.zeros((1, tok), jnp.int32)
    rank = jnp.ones((1, tok), jnp.int32)
    for b in range(blocks):
        near, rank_b = block_table(tables, b, d_ref[0])
        slot = jnp.where(lane >= starts[b], near, slot)
        rank = jnp.where(lane >= starts[b], rank_b, rank)
    src = sources(z_ref[0], parts)
    rank_at = z_ref[0] * own + lax.broadcasted_iota(jnp.int32, total.shape, 0)
    scale = adapter_alpha_scale / rank.astype(wide)
    total = jnp.where((rank_at < rank) & (lane < live_rows), total * scale, 0.0)
    lhs = jnp.concatenate([jnp.where(slot == j, total, 0.0).astype(half) for j in order], axis=0)
    room, kw = cots[0].shape
    for i in range(parts):
        cols = pl.ds(pl.multiple_of(src[i] * kw, kw), kw)
        acc_ref[:, cols] = mm(lhs[:, :room], cots[i][...], NN)

    @pl.when(live_rows > room)
    def _():
        for i in range(parts):
            cols = pl.ds(pl.multiple_of(src[i] * kw, kw), kw)
            acc_ref[:, cols] = acc_ref[:, cols] + mm(lhs[:, room:], rest_ref[i], NN)

    for k in range(per):
        for ref, at in ((keep_ref, k), (send_ref, per + k)):
            ref[k] = acc_ref[at * own : (at + 1) * own, :].astype(half)


def up_call(d, z, live, tables, hs, cots, rest, order):
    own, tok = hs[0].shape
    parts = len(cots)
    width = parts * cots[0].shape[1]
    shape = jax.ShapeDtypeStruct((len(order) // 2, own, width), half)
    return pl.pallas_call(
        functools.partial(up_kernel, order, parts, len(hs)),
        in_specs=[smem()] * 6 + [vmem()] * (len(hs) + len(cots) + 1),
        out_specs=[vmem()] * 2,
        out_shape=[shape, shape],
        scratch_shapes=[pltpu.VMEM((len(order) * own, width), wide)],
        compiler_params=kernel_params(24),
        cost_estimate=cost(2 * len(order) * own * tok * width, 4 * tok * width),
        name="up_grad",
    )(d, z, live, *tables, *hs, *cots, rest)


def up_plain(d, z, live, tables, hs, cots, rest, order):
    tenant, slot_of, rank_of = tables
    own, tok = hs[0].shape
    room = tok - rest.shape[1]
    pick = tenant[:, None] == jnp.arange(slot_of.shape[0])[None, :]
    near = jnp.bitwise_xor(jnp.sum(jnp.where(pick, slot_of[None, :], 0), axis=1), d)
    rank = jnp.sum(jnp.where(pick, rank_of[None, :], 0), axis=1)
    ends = jnp.cumsum(live)
    lane = jnp.arange(tok, dtype=jnp.int32)[None, :]
    mine = (lane >= (ends - live)[:, None]) & (lane < ends[:, None])
    slot = jnp.sum(jnp.where(mine, near[:, None], 0), axis=0)[None, :]
    rank = jnp.maximum(jnp.sum(jnp.where(mine, rank[:, None], 0), axis=0), 1)[None, :]
    total = sum(h.astype(wide) for h in hs)
    rank_at = z * own + jnp.arange(own, dtype=jnp.int32)[:, None]
    total = total * (adapter_alpha_scale / rank.astype(wide))
    total = jnp.where((rank_at < rank) & (lane < ends[-1]), total, 0.0)
    lhs = jnp.concatenate([jnp.where(slot == j, total, 0).astype(half) for j in order], axis=0)
    cot = [jnp.concatenate(cots, axis=1)]
    cot.append(jnp.where(ends[-1] > room, jnp.concatenate(list(rest), axis=1), 0))
    cot = jnp.concatenate(cot, axis=0)
    grads = mm(lhs, cot, NN).astype(half).reshape(len(order), own, cot.shape[1])
    return grads[: len(order) // 2], grads[len(order) // 2 :]


def base_kernel(parts, z_ref, live_ref, w_ref, *refs):
    cots, out_ref = refs[:-1], refs[-1]
    room, kw = cots[0].shape
    _, total = starts_of(live_ref)
    src = sources(z_ref[0], parts)
    blk = out_ref.shape[1] // pl.num_programs(0)
    cols = pl.ds(pl.multiple_of(pl.program_id(0) * blk, blk), blk)
    tile = min(256, room)
    for at in range(0, room, tile):

        @pl.when(at < total)
        def _(at=at):
            acc = None
            for i, cot in enumerate(cots):
                w = w_ref[cols, pl.ds(pl.multiple_of(src[i] * kw, kw), kw)]
                prod = mm(cot[at : at + tile, :], w, NT)
                acc = prod if acc is None else acc + prod
            out_ref[at : at + tile, cols] = acc


def base_call(z, live, w, cots, parts):
    room, kw = cots[0].shape
    width = w.shape[0]
    blk = min(512, width)
    return pl.pallas_call(
        functools.partial(base_kernel, parts),
        grid=(width // blk,),
        in_specs=[smem(), smem(), vmem()] + [vmem()] * len(cots),
        out_specs=vmem(),
        out_shape=jax.ShapeDtypeStruct((room, width), wide),
        compiler_params=kernel_params(16),
        cost_estimate=cost(2 * room * width * kw * len(cots), 4 * room * width),
        name="base",
    )(z, live, w, *cots)


def acts_kernel(parts, early, z_ref, live_ref, w_ref, u_ref, base_ref, rest_ref, *refs):
    cots, a_refs = refs[: parts - early], refs[parts - early : -3]
    out_ref, all_ref, acc_ref = refs[-3:]
    room, kw = cots[0].shape
    ranks = a_refs[0].shape[0]
    starts, total = starts_of(live_ref)
    src = sources(z_ref[0], parts)
    for i, ref in enumerate(a_refs):
        all_ref[i * ranks : (i + 1) * ranks, :] = ref[...]
    tok, blk = out_ref.shape
    cols = pl.ds(pl.multiple_of(pl.program_id(0) * blk, blk), blk)
    panels, _, lanes = acc_ref.shape

    def product(at, rows, acc, pieces):
        acc_u = mm(u_ref[at : at + rows, :], all_ref[...], NN)
        acc = acc_u if acc is None else acc + acc_u
        for i, piece in pieces:
            w = w_ref[cols, pl.ds(pl.multiple_of(src[i] * kw, kw), kw)]
            acc = acc + mm(piece, w, NT)
        for p in range(panels):
            acc_ref[p, at : at + rows, :] = acc[:, p * lanes : (p + 1) * lanes]

    tile = min(256, room)
    for at in range(0, room, tile):

        @pl.when(at < total)
        def _(at=at):
            first = base_ref[at : at + tile, cols] if early else None
            product(at, tile, first, [(early + i, cot[at : at + tile, :]) for i, cot in enumerate(cots)])

    @pl.when(total > room)
    def _():
        product(room, tok - room, None, [(i, rest_ref[i]) for i in range(parts)])

    blocks = live_ref.shape[0]
    blk_len = tok // blocks
    row = lax.broadcasted_iota(jnp.int32, (blk_len, lanes), 0)
    for b in range(blocks):
        for p in range(panels):
            piece = acc_ref[p, pl.ds(starts[b], blk_len), :]
            piece = jnp.where(row < live_ref[b], piece, 0.0)
            out_ref[b * blk_len : (b + 1) * blk_len, p * lanes : (p + 1) * lanes] = piece.astype(half)


def acts_call(z, live, w, u, base, cots, rest, downs):
    width, kfull = w.shape
    tok, every = u.shape
    ranks = downs[0].shape[0]
    blk = min(512, width)
    parts = rest.shape[0]
    return pl.pallas_call(
        functools.partial(acts_kernel, parts, parts - len(cots)),
        grid=(width // blk,),
        in_specs=[smem(), smem(), vmem(), vmem(), vmem(), vmem()]
        + [vmem()] * len(cots)
        + [pl.BlockSpec((ranks, blk), lambda i: (0, i))] * len(downs),
        out_specs=pl.BlockSpec((tok, blk), lambda i: (0, i)),
        out_shape=jax.ShapeDtypeStruct((tok, width), half),
        scratch_shapes=[
            pltpu.VMEM((every, blk), half),
            pltpu.VMEM((blk // 128, tok, 128), wide),
        ],
        compiler_params=kernel_params(24),
        cost_estimate=cost(0, 4 * tok),
        name="grad_acts",
    )(z, live, w, u, base, rest, *cots, *downs)


def together(*values):
    return lax.optimization_barrier(values)


def after(value, *others):
    return lax.optimization_barrier((value, *others))[0]


def shards(
    n_dp,
    n_tensor,
    activations,
    output_gradient,
    value_weight,
    adapter_down_factors,
    adapter_up_factors,
    down_first_moment,
    down_second_moment,
    up_first_moment,
    up_second_moment,
    block_tenant,
    block_live_tokens,
    tenant_storage_slot,
    tenant_adapter_rank,
):
    tok, width = activations.shape
    live = block_live_tokens
    slots = tenant_storage_slot.shape[0]
    assert adapter_down_factors.shape[0] == 1 and slots == n_dp and n_dp >= 4
    ranks = adapter_down_factors.shape[2]
    own_ranks = adapter_up_factors.shape[1]
    kw = output_gradient.shape[1]
    z = lax.axis_index("tensor").astype(jnp.int32)
    d = lax.axis_index("dp").astype(jnp.int32)
    z_one, d_one = z[None], d[None]
    order = bit_order(slots)
    levels = [1 << b for b in range(slots.bit_length() - 1)]
    tables = (block_tenant, tenant_storage_slot, tenant_adapter_rank)
    ring = line_ring(n_tensor)
    ring_pairs = [(ring[i], ring[(i + 1) % n_tensor]) for i in range(n_tensor)]

    def onward(v):
        return lax.ppermute(v, "tensor", ring_pairs)

    room = tok * 3 // 4
    own_b, first, rest = pack_call(live, adapter_up_factors, output_gradient, room, n_tensor)

    def rest_of(v):
        out = [v[0]]
        for _ in range(n_tensor - 1):
            out.append(onward(out[-1]))
        return jnp.stack(out)

    cots = [first, onward(first)]
    ups = [own_b, swap(own_b, "tensor", n_tensor, 1)]
    far = list(reversed(levels))
    downs = list(round_call(after(adapter_down_factors, first)))
    for bits in far[:-1]:
        downs = downs + [swap(v, "dp", n_dp, bits) for v in downs]


    rest = lax.cond(jnp.sum(live) > room, rest_of, lambda v: v, rest)

    cots[1], rest, *ups = together(cots[1], rest, *ups)
    cots.append(onward(cots[1]))
    bits = 2
    while bits < n_tensor:
        ups = ups + [swap(v, "tensor", n_tensor, bits) for v in ups]
        bits *= 2
    downs = [after(v, cots[1]) for v in downs]
    downs = downs + [swap(v, "dp", n_dp, far[-1]) for v in downs]
    hs = list(hidden_call(d_one, z_one, live, tables, activations, downs, order, n_tensor))

    cots[2], *both = together(cots[2], *hs, *ups)
    hs, ups = both[: len(hs)], both[len(hs) :]
    while len(cots) < n_tensor:
        cots.append(onward(cots[-1]))
    ups = [ordered_call(z_one, live, tables, ups)]
    for bits in far[:-1]:
        ups = ups + [swap(v, "dp", n_dp, bits) for v in ups]
    hs = [hs[0]] + [swap(hs[k], "tensor", n_tensor, k) for k in range(1, n_tensor)]
    early = 3 if kw % 128 == 0 and n_tensor > 3 else 0
    base = jnp.zeros((8, 128), wide)
    if early:
        base = base_call(z_one, live, value_weight, cots[:early], n_tensor)
    cots[-1], base, *both = together(cots[-1], base, *hs, *ups)
    hs, ups = both[: len(hs)], both[len(hs) :]
    ups = ups + [swap(v, "dp", n_dp, far[-1]) for v in ups]
    if kw % 128:
        at = jnp.array([ring.index(i) for i in range(n_tensor)], jnp.int32)
        away = (at[z] - at) % n_tensor
        in_order = lambda v: jnp.moveaxis(v[away], 0, 1).reshape(v.shape[1], n_tensor * kw)
        cots = [in_order(jnp.stack(cots))]
        rest = in_order(rest)[None]
    def other_sums(total, levels, *others):
        for bits in levels:
            n = total.shape[0] // 2
            got = after(swap(total[n:].astype(half), "dp", n_dp, bits), *others)
            total = total[:n] + got.astype(wide)
        return total[0]

    if own_ranks % 16:
        keep_up, send_up = up_plain(d, z, live, tables, hs, cots, rest, order)
    else:
        keep_up, send_up = up_call(d_one, z_one, live, tables, hs, cots, rest, order)
    got_up = swap(send_up, "dp", n_dp, 1)
    u, packed_u, count = upward_call(d_one, z_one, live, tables, cots, after(rest, send_up), ups, order, ranks)
    quarter = slots // 4
    keep_far, send_far = down_call(activations, u, ranks, 2 * quarter, quarter)
    got_far = swap(send_far, "dp", n_dp, 1)
    keep_near, send_near = down_call(activations, after(u, send_far), ranks, 0, quarter)
    sum_far = (keep_far.astype(wide) + after(got_far, send_near).astype(wide)).astype(half)
    got_far = swap(sum_far, "dp", n_dp, levels[1])
    got_near = swap(send_near, "dp", n_dp, 1)
    up_sum = keep_up.astype(wide) + after(got_up, sum_far).astype(wide)
    got_near = after(got_near, up_sum)
    grad_acts = acts_call(z_one, live, value_weight, after(packed_u, got_near), base, cots[early:], rest, downs)
    down_sum = keep_near.astype(wide) + got_near.astype(wide) + after(got_far, grad_acts).astype(wide)
    down_grad = other_sums(down_sum, levels[2:])[None] / count[None, :1, :ranks]
    new_down = moment_update_rule(adapter_down_factors, down_first_moment, down_second_moment, down_grad)
    up_grad = other_sums(up_sum, levels[1:], new_down[0])[None] / count[None, :1, :]
    new_up = moment_update_rule(adapter_up_factors, up_first_moment, up_second_moment, up_grad)
    return (grad_acts, *new_down, *new_up)


def solution(mesh):
    tokens = P(("groups", "dp"), "tensor")
    factors = P(("groups", "dp"), "tensor", None)
    placed = (tokens, tokens, P("tensor", None), *([factors] * 6), P(("groups", "dp")), P(("groups", "dp")), P("groups"), P("groups"))
    return jax.shard_map(
        functools.partial(shards, mesh.shape["dp"], mesh.shape["tensor"]),
        mesh=mesh,
        in_specs=placed,
        out_specs=(tokens, *([factors] * 6)),
        check_vma=False,
    )
```

```python
import functools

import jax
import jax.numpy as jnp
from jax import lax
from jax.experimental import pallas as pl
from jax.experimental.pallas import tpu as pltpu
from jax.sharding import PartitionSpec as P

adapter_alpha_scale = 16.0
beta_one = 0.9
beta_two = 0.999
adam_eps = 1e-08
learn_rate = 0.001
adam_step = 10
half = jnp.bfloat16
wide = jnp.float32
MIB = 1 << 20
NT = (((1,), (1,)), ((), ()))
TN = (((0,), (0,)), ((), ()))
NN = (((1,), (0,)), ((), ()))


def mm(a, b, dims):
    return lax.dot_general(a, b, dims, preferred_element_type=wide)


def moment_update_rule(param, first, second, grad):
    new_first = beta_one * first + (1.0 - beta_one) * grad
    new_second = beta_two * second + (1.0 - beta_two) * grad * grad
    fixed_first = new_first / (1.0 - beta_one**adam_step)
    fixed_second = new_second / (1.0 - beta_two**adam_step)
    return (
        param - learn_rate * fixed_first / (jnp.sqrt(fixed_second) + adam_eps),
        new_first,
        new_second,
    )


def bit_order(n):
    if n == 1:
        return [0]
    inner = [2 * i for i in bit_order(n // 2)]
    return inner + [i + 1 for i in inner]


def paired(order):
    q = len(order) // 4
    return order[:q] + order[2 * q : 3 * q] + order[q : 2 * q] + order[3 * q :]


def line_ring(n):
    return [0] + list(range(1, n, 2)) + list(range(n - 2 + n % 2, 0, -2))


def swap(v, axis, n, bits):
    return lax.ppermute(v, axis, [(i, i ^ bits) for i in range(n)])


def kernel_params(mib):
    return pltpu.CompilerParams(vmem_limit_bytes=mib * MIB)


def cost(flops, nbytes):
    return pl.CostEstimate(flops=int(flops), bytes_accessed=int(nbytes), transcendentals=0)


def block_table(refs, b, d):
    tenant_ref, slot_ref, rank_ref = refs
    tenant = tenant_ref[b]
    return jnp.bitwise_xor(slot_ref[tenant], d), rank_ref[tenant]


def inverse_rank(rank, shape):
    return adapter_alpha_scale / jnp.full(shape, rank, jnp.int32).astype(wide)


def sources(z, n):
    ring = line_ring(n)
    out = []
    for i in range(n):
        came = [ring[(ring.index(k) - i) % n] for k in range(n)]
        at = came[0]
        for k in range(1, n):
            at = jnp.where(z == k, came[k], at)
        out.append(at)
    return out


def smem():
    return pl.BlockSpec(memory_space=pltpu.SMEM)


def resident(a):
    return pl.BlockSpec(a.shape, lambda *_, n=len(a.shape): (0,) * n)


def vmem():
    return pl.BlockSpec(memory_space=pltpu.VMEM)


def starts_of(live_ref):
    starts, at = [], 0
    for b in range(live_ref.shape[0]):
        starts.append(at)
        at = at + live_ref[b]
    return starts, at


def stage_kernel(from_ref, to_ref, sem):
    copy = pltpu.make_async_copy(from_ref, to_ref, sem)
    copy.start()
    copy.wait()


def stage_call(a):
    return pl.pallas_call(
        stage_kernel,
        in_specs=[pl.BlockSpec(memory_space=pl.ANY)],
        out_specs=vmem(),
        out_shape=jax.ShapeDtypeStruct(a.shape, a.dtype),
        scratch_shapes=[pltpu.SemaphoreType.DMA],
        compiler_params=kernel_params(16),
        cost_estimate=cost(0, 4 * a.size),
        name="stage",
    )(a)


def round_kernel(a_ref, low_ref, high_ref):
    turned = a_ref[0].T.astype(half)
    low_ref[...] = turned[: low_ref.shape[0]]
    high_ref[...] = turned[low_ref.shape[0] :]


def round_call(a):
    _, width, ranks = a.shape
    blk = width
    return pl.pallas_call(
        round_kernel,
        grid=(width // blk,),
        in_specs=[pl.BlockSpec((1, blk, ranks), lambda i: (0, i, 0))],
        out_specs=[pl.BlockSpec((ranks // 2, blk), lambda i: (0, i))] * 2,
        out_shape=[jax.ShapeDtypeStruct((ranks // 2, width), half)] * 2,
        compiler_params=kernel_params(16),
        cost_estimate=cost(0, 6 * a.size),
        name="round_factors",
    )(a)


def pack_kernel(live_ref, b_ref, cot_ref, up_ref, first_ref, rest_ref, all_ref):
    blocks = live_ref.shape[0]
    blk_len = cot_ref.shape[0] // blocks
    starts, _ = starts_of(live_ref)
    all_ref[...] = jnp.zeros_like(all_ref)
    panels, _, lanes = all_ref.shape
    row = lax.broadcasted_iota(jnp.int32, (blk_len, lanes), 0)
    for b in range(blocks):
        for p in range(panels):
            piece = cot_ref[b * blk_len : (b + 1) * blk_len, p * lanes : (p + 1) * lanes].astype(wide)
            all_ref[p, pl.ds(starts[b], blk_len), :] = jnp.where(row < live_ref[b], piece, 0.0)
    room = first_ref.shape[0]
    for p in range(panels):
        cols = slice(p * lanes, (p + 1) * lanes)
        first_ref[:, cols] = all_ref[p, :room, :].astype(half)
        rest_ref[0, :, cols] = all_ref[p, room:, :].astype(half)
    up_ref[...] = b_ref[0].astype(half)


def pack_call(live, b, cot, room, copies):
    tok, kw = cot.shape
    shapes = [
        jax.ShapeDtypeStruct(b.shape[1:], half),
        jax.ShapeDtypeStruct((room, kw), half),
        jax.ShapeDtypeStruct((copies, tok - room, kw), half),
    ]
    specs = [resident(v) for v in shapes[:-1]] + [pl.BlockSpec((1, tok - room, kw), lambda i: (0, 0, 0))]
    return pl.pallas_call(
        pack_kernel,
        grid=(1,),
        in_specs=[smem(), resident(b), resident(cot)],
        out_specs=specs,
        out_shape=shapes,
        scratch_shapes=[pltpu.VMEM((kw // min(kw, 128), tok, min(kw, 128)), wide)],
        compiler_params=kernel_params(56),
        cost_estimate=cost(0, 4 * tok * kw + 6 * b.size),
        name="pack",
    )(live, b, cot)


def ordered_kernel(z_ref, live_ref, tenant_ref, slot_ref, *refs):
    out_ref = refs[-1]
    own = refs[0].shape[0]
    for k, ref in enumerate(refs[:-1]):
        at = pl.multiple_of(jnp.bitwise_xor(z_ref[0], k) * own, own)
        out_ref[pl.ds(at, own), :] = ref[...]
    ranks = own * (len(refs) - 1)
    shape = (out_ref.shape[0] - ranks, out_ref.shape[1])
    row, lane = lax.broadcasted_iota(jnp.int32, shape, 0), lax.broadcasted_iota(jnp.int32, shape, 1)
    tail = jnp.zeros(shape, jnp.int32)
    for q in range(slot_ref.shape[0]):
        count = jnp.int32(0)
        for b in range(live_ref.shape[0]):
            count = count + jnp.where(slot_ref[tenant_ref[b]] == q, live_ref[b], 0)
        digit = jnp.where(row == 0, count // 32, jnp.where(row == 1, count % 32, 0))
        tail = jnp.where(lane == q, digit, tail)
    out_ref[ranks:, :] = tail.astype(wide).astype(half)


def ordered_call(z, live, tables, pieces, tail_rows=16):
    own, cols = pieces[0].shape
    n = len(pieces)
    tenant, slot_of, _ = tables
    if own % 16:
        rows = jnp.stack(pieces)[jnp.bitwise_xor(z[0], jnp.arange(n))].reshape(n * own, cols)
        pick = tenant[:, None] == jnp.arange(slot_of.shape[0])[None, :]
        slot = jnp.sum(jnp.where(pick, slot_of[None, :], 0), axis=1)
        mine = slot[:, None] == jnp.arange(slot_of.shape[0])[None, :]
        counts = jnp.sum(jnp.where(mine, live[:, None], 0), axis=0)
        tail = jnp.stack([counts // 32, counts % 32]).astype(wide).astype(half)
        return jnp.concatenate([rows, jnp.pad(tail, ((0, tail_rows - 2), (0, cols - slot_of.shape[0])))], axis=0)
    return pl.pallas_call(
        ordered_kernel,
        in_specs=[smem()] * 4 + [vmem()] * n,
        out_specs=vmem(),
        out_shape=jax.ShapeDtypeStruct((n * own + tail_rows, cols), half),
        compiler_params=kernel_params(16),
        cost_estimate=cost(0, 4 * n * own * cols),
        name="ordered",
    )(z, live, tenant, slot_of, *pieces)


def hidden_kernel(order, groups, d_ref, z_ref, live_ref, *refs):
    tables, x_ref, a_refs, out_refs = refs[:3], refs[3], refs[4 : -4 - groups], refs[-4 - groups : -4]
    all_ref, prod_ref, rows_ref, flat_ref = refs[-4:]
    ranks = rows_ref.shape[1]
    step = pl.program_id(0)

    @pl.when(step == 0)
    def _():
        rows = a_refs[0].shape[0]
        for i, ref in enumerate(a_refs):
            all_ref[i * rows : (i + 1) * rows, :] = ref[...]

    blk = prod_ref.shape[0]
    prod_ref[...] = mm(x_ref[pl.ds(pl.multiple_of(step * blk, blk), blk), :], all_ref[...], NT)
    blocks = live_ref.shape[0]
    blk_len = rows_ref.shape[0] // blocks
    per_step = blk // blk_len
    first = step * per_step
    start = jnp.int32(0)
    for b in range(blocks):
        start = start + jnp.where(b < first, live_ref[b], 0)
    for b in range(per_step):
        near, _ = block_table(tables, first + b, d_ref[0])
        at = jnp.int32(0)
        for i, j in enumerate(order):
            at = jnp.where(near == j, i, at)
        cols = pl.ds(pl.multiple_of(at * ranks, ranks), ranks)
        rows_ref[pl.ds(start, blk_len), :] = prod_ref[b * blk_len : (b + 1) * blk_len, cols]
        start = start + live_ref[first + b]

    @pl.when(step == pl.num_programs(0) - 1)
    def _():
        flat_ref[...] = rows_ref[...].T
        own = ranks // groups
        for k, out_ref in enumerate(out_refs):
            at = pl.multiple_of(jnp.bitwise_xor(z_ref[0], k) * own, own)
            out_ref[...] = flat_ref[pl.ds(at, own), :].astype(half)


def hidden_call(d, z, live, tables, x, downs, order, groups):
    tok, width = x.shape
    every = sum(a.shape[0] for a in downs)
    ranks = every // len(order)
    blk = min(256, tok)
    own = ranks // groups
    shape = jax.ShapeDtypeStruct((own, tok), half)
    return pl.pallas_call(
        functools.partial(hidden_kernel, order, groups),
        grid=(tok // blk,),
        in_specs=[smem()] * 6
        + [vmem()] * (1 + len(downs)),
        out_specs=[resident(shape)] * groups,
        out_shape=[shape] * groups,
        scratch_shapes=[
            pltpu.VMEM((every, width), half),
            pltpu.VMEM((blk, every), wide),
            pltpu.VMEM((tok, ranks), wide),
            pltpu.VMEM((ranks, tok), wide),
        ],
        compiler_params=kernel_params(24),
        cost_estimate=cost(0, 4 * tok),
        name="hidden",
    )(d, z, live, *tables, x, *downs)


def upward_kernel(order, parts, d_ref, z_ref, live_ref, *refs):
    tables, cots, rest_ref = refs[:3], refs[3 : 3 + parts], refs[3 + parts]
    b_refs = refs[4 + parts : -6]
    full_ref, packed_ref, count_ref, all_ref, acc_ref, rows_ref = refs[-6:]
    ranks = acc_ref.shape[2]
    room, kw = cots[0].shape
    count = jnp.zeros((1, b_refs[0].shape[1]), wide)
    for i, ref in enumerate(b_refs):
        all_ref[i * ranks : (i + 1) * ranks, :] = ref[:ranks, :]
        tail = ref[ranks:, :].astype(wide)
        count = count + tail[0:1] * 32.0 + tail[1:2]
    lane = lax.broadcasted_iota(jnp.int32, count.shape, 1)
    count = jnp.sum(jnp.where(lane == d_ref[0], count, 0.0), axis=1, keepdims=True)
    count_ref[...] = jnp.broadcast_to(jnp.maximum(count, 1.0), count_ref.shape)

    src = sources(z_ref[0], parts)

    def product(at, rows, pieces):
        acc = None
        for i, piece in enumerate(pieces):
            cols = pl.ds(pl.multiple_of(src[i] * kw, kw), kw)
            prod = mm(piece, all_ref[:, cols], NT)
            acc = prod if acc is None else acc + prod
        for i in range(len(order)):
            acc_ref[i, at : at + rows, :] = acc[:, i * ranks : (i + 1) * ranks]

    product(0, room, [ref[...] for ref in cots])
    starts, total = starts_of(live_ref)

    @pl.when(total > room)
    def _():
        product(room, rest_ref.shape[1], [rest_ref[i] for i in range(parts)])

    blocks = live_ref.shape[0]
    blk_len = full_ref.shape[0] // blocks
    panels = paired(order)
    rank_at = lax.broadcasted_iota(jnp.int32, (1, ranks), 1)
    row = lax.broadcasted_iota(jnp.int32, (blk_len, ranks), 0)
    for b in range(blocks):
        near, rank = block_table(tables, b, d_ref[0])
        scale = jnp.where(rank_at < rank, inverse_rank(rank, (1, ranks)), 0.0)
        for i, j in enumerate(order):
            piece = acc_ref[i, pl.ds(starts[b], blk_len), :] * jnp.where(near == j, scale, 0.0)
            piece = jnp.where(row < live_ref[b], piece, 0.0)
            at = panels.index(j)
            full_ref[b * blk_len : (b + 1) * blk_len, at * ranks : (at + 1) * ranks] = piece.astype(half)
            rows_ref[i, pl.ds(starts[b], blk_len), :] = piece
    for i in range(len(order)):
        packed_ref[:, i * ranks : (i + 1) * ranks] = rows_ref[i].astype(half)


def upward_call(d, z, live, tables, cots, rest, ups, order, ranks):
    value_width = ups[0].shape[1]
    every = len(ups) * ranks
    tok = cots[0].shape[0] + rest.shape[1]
    shape = jax.ShapeDtypeStruct((tok, every), half)
    return pl.pallas_call(
        functools.partial(upward_kernel, order, len(cots)),
        in_specs=[smem()] * 6 + [vmem()] * (len(cots) + 1 + len(ups)),
        out_specs=[vmem()] * 3,
        out_shape=[shape, shape, jax.ShapeDtypeStruct((8, value_width), wide)],
        scratch_shapes=[
            pltpu.VMEM((every, value_width), half),
            pltpu.VMEM((len(ups), tok, ranks), wide),
            pltpu.VMEM((len(ups), tok, ranks), wide),
        ],
        compiler_params=kernel_params(24),
        cost_estimate=cost(2 * tok * value_width * every, 2 * (tok * value_width + 2 * every * value_width)),
        name="upward",
    )(d, z, live, *tables, *cots, rest, *ups)


def down_kernel(ranks, first, x_ref, u_ref, keep_ref, send_ref):
    count, blk, _ = keep_ref.shape
    x = x_ref[:, pl.ds(pl.multiple_of(pl.program_id(0) * blk, blk), blk)]
    acc = mm(x, u_ref[:, first * ranks : (first + 2 * count) * ranks], TN)
    for i in range(count):
        keep_ref[i] = acc[:, i * ranks : (i + 1) * ranks].astype(half)
        send_ref[i] = acc[:, (count + i) * ranks : (count + i + 1) * ranks].astype(half)


def down_call(x, u, ranks, first, count):
    tok, width = x.shape
    blk = min(512, width)
    shape = jax.ShapeDtypeStruct((count, width, ranks), half)
    return pl.pallas_call(
        functools.partial(down_kernel, ranks, first),
        grid=(width // blk,),
        in_specs=[vmem(), vmem()],
        out_specs=[pl.BlockSpec((count, blk, ranks), lambda i: (0, i, 0))] * 2,
        out_shape=[shape, shape],
        compiler_params=kernel_params(24),
        cost_estimate=cost(0, 4 * tok),
        name="down_grad",
    )(x, u)


def up_kernel(order, parts, n_hs, d_ref, z_ref, live_ref, *refs):
    tables, hs = refs[:3], refs[3 : 3 + n_hs]
    cots, rest_ref = refs[3 + n_hs : 3 + n_hs + parts], refs[3 + n_hs + parts]
    keep_ref, send_ref, acc_ref = refs[-3:]
    own, tok = hs[0].shape
    per = len(order) // 2
    blocks = live_ref.shape[0]
    total = hs[0][...].astype(wide)
    for h in hs[1:]:
        total = total + h[...].astype(wide)
    starts, live_rows = starts_of(live_ref)
    lane = lax.broadcasted_iota(jnp.int32, (1, tok), 1)
    slot = jnp.zeros((1, tok), jnp.int32)
    rank = jnp.ones((1, tok), jnp.int32)
    for b in range(blocks):
        near, rank_b = block_table(tables, b, d_ref[0])
        slot = jnp.where(lane >= starts[b], near, slot)
        rank = jnp.where(lane >= starts[b], rank_b, rank)
    src = sources(z_ref[0], parts)
    rank_at = z_ref[0] * own + lax.broadcasted_iota(jnp.int32, total.shape, 0)
    scale = adapter_alpha_scale / rank.astype(wide)
    total = jnp.where((rank_at < rank) & (lane < live_rows), total * scale, 0.0)
    lhs = jnp.concatenate([jnp.where(slot == j, total, 0.0).astype(half) for j in order], axis=0)
    room, kw = cots[0].shape
    for i in range(parts):
        cols = pl.ds(pl.multiple_of(src[i] * kw, kw), kw)
        acc_ref[:, cols] = mm(lhs[:, :room], cots[i][...], NN)

    @pl.when(live_rows > room)
    def _():
        for i in range(parts):
            cols = pl.ds(pl.multiple_of(src[i] * kw, kw), kw)
            acc_ref[:, cols] = acc_ref[:, cols] + mm(lhs[:, room:], rest_ref[i], NN)

    for k in range(per):
        for ref, at in ((keep_ref, k), (send_ref, per + k)):
            ref[k] = acc_ref[at * own : (at + 1) * own, :].astype(half)


def up_call(d, z, live, tables, hs, cots, rest, order):
    own, tok = hs[0].shape
    parts = len(cots)
    width = parts * cots[0].shape[1]
    shape = jax.ShapeDtypeStruct((len(order) // 2, own, width), half)
    return pl.pallas_call(
        functools.partial(up_kernel, order, parts, len(hs)),
        in_specs=[smem()] * 6 + [vmem()] * (len(hs) + len(cots) + 1),
        out_specs=[vmem()] * 2,
        out_shape=[shape, shape],
        scratch_shapes=[pltpu.VMEM((len(order) * own, width), wide)],
        compiler_params=kernel_params(24),
        cost_estimate=cost(2 * len(order) * own * tok * width, 4 * tok * width),
        name="up_grad",
    )(d, z, live, *tables, *hs, *cots, rest)


def up_plain(d, z, live, tables, hs, cots, rest, order):
    tenant, slot_of, rank_of = tables
    own, tok = hs[0].shape
    room = tok - rest.shape[1]
    pick = tenant[:, None] == jnp.arange(slot_of.shape[0])[None, :]
    near = jnp.bitwise_xor(jnp.sum(jnp.where(pick, slot_of[None, :], 0), axis=1), d)
    rank = jnp.sum(jnp.where(pick, rank_of[None, :], 0), axis=1)
    ends = jnp.cumsum(live)
    lane = jnp.arange(tok, dtype=jnp.int32)[None, :]
    mine = (lane >= (ends - live)[:, None]) & (lane < ends[:, None])
    slot = jnp.sum(jnp.where(mine, near[:, None], 0), axis=0)[None, :]
    rank = jnp.maximum(jnp.sum(jnp.where(mine, rank[:, None], 0), axis=0), 1)[None, :]
    total = sum(h.astype(wide) for h in hs)
    rank_at = z * own + jnp.arange(own, dtype=jnp.int32)[:, None]
    total = total * (adapter_alpha_scale / rank.astype(wide))
    total = jnp.where((rank_at < rank) & (lane < ends[-1]), total, 0.0)
    lhs = jnp.concatenate([jnp.where(slot == j, total, 0).astype(half) for j in order], axis=0)
    cot = [jnp.concatenate(cots, axis=1)]
    cot.append(jnp.where(ends[-1] > room, jnp.concatenate(list(rest), axis=1), 0))
    cot = jnp.concatenate(cot, axis=0)
    grads = mm(lhs, cot, NN).astype(half).reshape(len(order), own, cot.shape[1])
    return grads[: len(order) // 2], grads[len(order) // 2 :]


def base_kernel(parts, z_ref, live_ref, w_ref, *refs):
    cots, out_ref = refs[:-1], refs[-1]
    room, kw = cots[0].shape
    _, total = starts_of(live_ref)
    src = sources(z_ref[0], parts)
    blk = out_ref.shape[1] // pl.num_programs(0)
    cols = pl.ds(pl.multiple_of(pl.program_id(0) * blk, blk), blk)
    tile = min(256, room)
    for at in range(0, room, tile):

        @pl.when(at < total)
        def _(at=at):
            acc = None
            for i, cot in enumerate(cots):
                w = w_ref[cols, pl.ds(pl.multiple_of(src[i] * kw, kw), kw)]
                prod = mm(cot[at : at + tile, :], w, NT)
                acc = prod if acc is None else acc + prod
            out_ref[at : at + tile, cols] = acc


def base_call(z, live, w, cots, parts):
    room, kw = cots[0].shape
    width = w.shape[0]
    blk = min(512, width)
    return pl.pallas_call(
        functools.partial(base_kernel, parts),
        grid=(width // blk,),
        in_specs=[smem(), smem(), vmem()] + [vmem()] * len(cots),
        out_specs=vmem(),
        out_shape=jax.ShapeDtypeStruct((room, width), wide),
        compiler_params=kernel_params(16),
        cost_estimate=cost(2 * room * width * kw * len(cots), 4 * room * width),
        name="base",
    )(z, live, w, *cots)


def acts_kernel(parts, early, z_ref, live_ref, w_ref, u_ref, base_ref, rest_ref, *refs):
    cots, a_refs = refs[: parts - early], refs[parts - early : -3]
    out_ref, all_ref, acc_ref = refs[-3:]
    room, kw = cots[0].shape
    ranks = a_refs[0].shape[0]
    starts, total = starts_of(live_ref)
    src = sources(z_ref[0], parts)
    for i, ref in enumerate(a_refs):
        all_ref[i * ranks : (i + 1) * ranks, :] = ref[...]
    tok, blk = out_ref.shape
    cols = pl.ds(pl.multiple_of(pl.program_id(0) * blk, blk), blk)
    panels, _, lanes = acc_ref.shape

    def product(at, rows, acc, pieces):
        acc_u = mm(u_ref[at : at + rows, :], all_ref[...], NN)
        acc = acc_u if acc is None else acc + acc_u
        for i, piece in pieces:
            w = w_ref[cols, pl.ds(pl.multiple_of(src[i] * kw, kw), kw)]
            acc = acc + mm(piece, w, NT)
        for p in range(panels):
            acc_ref[p, at : at + rows, :] = acc[:, p * lanes : (p + 1) * lanes]

    tile = min(256, room)
    for at in range(0, room, tile):

        @pl.when(at < total)
        def _(at=at):
            first = base_ref[at : at + tile, cols] if early else None
            product(at, tile, first, [(early + i, cot[at : at + tile, :]) for i, cot in enumerate(cots)])

    @pl.when(total > room)
    def _():
        product(room, tok - room, None, [(i, rest_ref[i]) for i in range(parts)])

    blocks = live_ref.shape[0]
    blk_len = tok // blocks
    row = lax.broadcasted_iota(jnp.int32, (blk_len, lanes), 0)
    for b in range(blocks):
        for p in range(panels):
            piece = acc_ref[p, pl.ds(starts[b], blk_len), :]
            piece = jnp.where(row < live_ref[b], piece, 0.0)
            out_ref[b * blk_len : (b + 1) * blk_len, p * lanes : (p + 1) * lanes] = piece.astype(half)


def acts_call(z, live, w, u, base, cots, rest, downs):
    width, kfull = w.shape
    tok, every = u.shape
    ranks = downs[0].shape[0]
    blk = min(512, width)
    parts = rest.shape[0]
    return pl.pallas_call(
        functools.partial(acts_kernel, parts, parts - len(cots)),
        grid=(width // blk,),
        in_specs=[smem(), smem(), vmem(), vmem(), vmem(), vmem()]
        + [vmem()] * len(cots)
        + [pl.BlockSpec((ranks, blk), lambda i: (0, i))] * len(downs),
        out_specs=pl.BlockSpec((tok, blk), lambda i: (0, i)),
        out_shape=jax.ShapeDtypeStruct((tok, width), half),
        scratch_shapes=[
            pltpu.VMEM((every, blk), half),
            pltpu.VMEM((blk // 128, tok, 128), wide),
        ],
        compiler_params=kernel_params(24),
        cost_estimate=cost(0, 4 * tok),
        name="grad_acts",
    )(z, live, w, u, base, rest, *cots, *downs)


def together(*values):
    return lax.optimization_barrier(values)


def after(value, *others):
    return lax.optimization_barrier((value, *others))[0]


def shards(
    n_dp,
    n_tensor,
    activations,
    output_gradient,
    value_weight,
    adapter_down_factors,
    adapter_up_factors,
    down_first_moment,
    down_second_moment,
    up_first_moment,
    up_second_moment,
    block_tenant,
    block_live_tokens,
    tenant_storage_slot,
    tenant_adapter_rank,
):
    tok, width = activations.shape
    live = block_live_tokens
    slots = tenant_storage_slot.shape[0]
    assert adapter_down_factors.shape[0] == 1 and slots == n_dp and n_dp >= 4
    ranks = adapter_down_factors.shape[2]
    own_ranks = adapter_up_factors.shape[1]
    kw = output_gradient.shape[1]
    z = lax.axis_index("tensor").astype(jnp.int32)
    d = lax.axis_index("dp").astype(jnp.int32)
    z_one, d_one = z[None], d[None]
    order = bit_order(slots)
    levels = [1 << b for b in range(slots.bit_length() - 1)]
    tables = (block_tenant, tenant_storage_slot, tenant_adapter_rank)
    ring = line_ring(n_tensor)
    ring_pairs = [(ring[i], ring[(i + 1) % n_tensor]) for i in range(n_tensor)]

    def onward(v):
        return lax.ppermute(v, "tensor", ring_pairs)

    room = tok * 3 // 4
    own_b, first, rest = pack_call(live, adapter_up_factors, output_gradient, room, n_tensor)

    def rest_of(v):
        out = [v[0]]
        for _ in range(n_tensor - 1):
            out.append(onward(out[-1]))
        return jnp.stack(out)

    cots = [first, onward(first)]
    ups = [own_b, swap(own_b, "tensor", n_tensor, 1)]
    far = list(reversed(levels))
    downs = list(round_call(after(adapter_down_factors, first)))
    for bits in far[:-1]:
        downs = downs + [swap(v, "dp", n_dp, bits) for v in downs]


    rest = lax.cond(jnp.sum(live) > room, rest_of, lambda v: v, rest)

    cots[1], rest, *ups = together(cots[1], rest, *ups)
    cots.append(onward(cots[1]))
    bits = 2
    while bits < n_tensor:
        ups = ups + [swap(v, "tensor", n_tensor, bits) for v in ups]
        bits *= 2
    downs = [after(v, cots[1]) for v in downs]
    downs = downs + [swap(v, "dp", n_dp, far[-1]) for v in downs]
    hs = list(hidden_call(d_one, z_one, live, tables, activations, downs, order, n_tensor))

    cots[2], *both = together(cots[2], *hs, *ups)
    hs, ups = both[: len(hs)], both[len(hs) :]
    while len(cots) < n_tensor:
        cots.append(onward(cots[-1]))
    ups = [ordered_call(z_one, live, tables, ups)]
    for bits in far[:-1]:
        ups = ups + [swap(v, "dp", n_dp, bits) for v in ups]
    early = 3 if kw % 128 == 0 and n_tensor > 3 else 0
    base = jnp.zeros((8, 128), wide)
    if early:
        base = base_call(z_one, live, value_weight, cots[:early], n_tensor)
    cots[-1], base, *ups = together(cots[-1], base, *ups)
    ups = ups + [swap(v, "dp", n_dp, far[-1]) for v in ups]
    if kw % 128:
        at = jnp.array([ring.index(i) for i in range(n_tensor)], jnp.int32)
        away = (at[z] - at) % n_tensor
        in_order = lambda v: jnp.moveaxis(v[away], 0, 1).reshape(v.shape[1], n_tensor * kw)
        cots = [in_order(jnp.stack(cots))]
        rest = in_order(rest)[None]
    def other_sums(total, levels, *others):
        for bits in levels:
            n = total.shape[0] // 2
            got = after(swap(total[n:].astype(half), "dp", n_dp, bits), *others)
            total = total[:n] + got.astype(wide)
        return total[0]

    u, packed_u, count = upward_call(d_one, z_one, live, tables, cots, rest, ups, order, ranks)
    quarter = slots // 4
    keep_far, send_far = down_call(activations, u, ranks, 2 * quarter, quarter)
    got_far = swap(send_far, "dp", n_dp, 1)
    keep_near, send_near = down_call(activations, after(u, send_far), ranks, 0, quarter)
    sum_far = (keep_far.astype(wide) + after(got_far, send_near).astype(wide)).astype(half)
    got_far = swap(sum_far, "dp", n_dp, levels[1])
    hs = [after(v, sum_far) for v in hs]
    hs = [hs[0]] + [swap(hs[k], "tensor", n_tensor, k) for k in range(1, n_tensor)]
    got_near = swap(send_near, "dp", n_dp, 1)
    got_near = after(got_near, sum_far)
    grad_acts = acts_call(z_one, live, value_weight, after(packed_u, got_near), base, cots[early:], rest, downs)
    hs[0] = after(hs[0], grad_acts)
    if own_ranks % 16:
        keep_up, send_up = up_plain(d, z, live, tables, hs, cots, rest, order)
    else:
        keep_up, send_up = up_call(d_one, z_one, live, tables, hs, cots, rest, order)
    got_up = swap(send_up, "dp", n_dp, 1)
    up_sum = keep_up.astype(wide) + got_up.astype(wide)
    down_sum = keep_near.astype(wide) + got_near.astype(wide) + after(got_far, up_sum).astype(wide)
    down_grad = other_sums(down_sum, levels[2:])[None] / count[None, :1, :ranks]
    new_down = moment_update_rule(adapter_down_factors, down_first_moment, down_second_moment, down_grad)
    up_grad = other_sums(up_sum, levels[1:], new_down[0])[None] / count[None, :1, :]
    new_up = moment_update_rule(adapter_up_factors, up_first_moment, up_second_moment, up_grad)
    return (grad_acts, *new_down, *new_up)


def solution(mesh):
    tokens = P(("groups", "dp"), "tensor")
    factors = P(("groups", "dp"), "tensor", None)
    placed = (tokens, tokens, P("tensor", None), *([factors] * 6), P(("groups", "dp")), P(("groups", "dp")), P("groups"), P("groups"))
    return jax.shard_map(
        functools.partial(shards, mesh.shape["dp"], mesh.shape["tensor"]),
        mesh=mesh,
        in_specs=placed,
        out_specs=(tokens, *([factors] * 6)),
        check_vma=False,
    )
```
